32 devices in a mesh: stripe: 2 (over x), tile: 16 (over z, y, core).
Axes of the slice: x: 2, y: 2, z: 4, core: 2. Of those that a mesh axis runs over, the one named last changes fastest.
Arguments:
- mask_tiles: float32 [32, 1024, 1024], P(('stripe', 'tile')), parts along dimension 0, may hold values from -1 to 1
- target_grid: float32 [32, 16384], P(('stripe', 'tile')), parts along dimension 0, may hold values from 0 to 1
- kernels: float32 [16, 2, 24, 64, 96], P('tile'), may hold values from -48 to 48
- kern_weight: float32 [24], replicated, may hold values from 0.05 to 1
- owner_list: int32 [32, 1], P('stripe'), parts along dimension 0, may hold values from 0 to 15, as said below
Outputs:
- mask_out: float32 [32, 1024, 1024], P(('stripe', 'tile')), parts along dimension 0
- owner_error: float32 [32], P(('stripe', 'tile')), parts along dimension 0
The draws below stay inside these ranges and needn't reach their ends.
There are 2 independent parts, one for each index of `stripe`. The reference program is written for one: setup_inputs(seed, part) draws one part's arguments, and reference() takes and returns one part's arrays. A program takes and returns all parts, laid end to end along the dimension named above; an argument that names none is the same for every part. Nothing has to cross between parts.
Inputs may be any that keep to these rules, and one draw needn't show every extreme that they name: `owner_list`: every owner is named by 0 to 2 tiles of a stripe, and some owner by exactly 2.
All inputs are finite; a program needn't handle non-finite values.
Results may differ from the reference program's by a relative error of at most 0.0001.
Values sent between devices are 32-bit elements; how exact they have to be, the bound alone decides.
A program may use at most 128 MiB of HBM per device.

```python
import math
import jax
import jax.numpy as jnp
from jax import lax

TILE_PX = 1024
AMBIT = 256
KERN = 24
ITERS = 1
DIFF_STEPS = 2
WIN = 1536
FREQ_X = 96
FREQ_Y = 64
GRID_X = 192
GRID_Y = 128
CORE_X = 128
TILES = 16
OWNERS = 16


def draw_owner_list(key, part):
    shuffled = jax.random.permutation(jax.random.fold_in(key, 11), TILES).astype(jnp.int32)
    pair_bits = jax.random.randint(jax.random.fold_in(key, 12), (TILES,), 0, 2, dtype=jnp.int32)
    positions = jnp.arange(TILES, dtype=jnp.int32)
    pair_bits = jnp.where(positions == 1, 1, pair_bits)
    odd_flags = positions % 2
    source_pos = positions - odd_flags * pair_bits
    return shuffled[source_pos][:, None]


def level_of(rng, shape, shards, least, high):
    def one(position, shards_of):
        steps = jax.random.uniform(jax.random.fold_in(jax.random.fold_in(rng, 6), position), (shards_of,), jnp.float32, least / len(shards), high / len(shards))
        return jnp.repeat(jnp.exp(steps), shape[position] // shards_of).reshape((-1,) + (1,) * (len(shape) - position - 1))

    loudness = one(*shards[0])
    for cut in shards[1:]:
        loudness = loudness * one(*cut)
    return loudness


def noise(own_key, shape, deviation, limit, pieces=(), held_as=jnp.bfloat16):
    result = jax.random.normal(own_key, shape, jnp.float32) * deviation
    if len(pieces) > 0:
        result = level_of(own_key, shape, pieces, -0.22, 0.18) * result
    return jnp.clip(result, min=-limit, max=limit).astype(held_as)


def setup_inputs(seed: int = 0, part: int = 0) -> dict:
    key_list = jax.random.split(jax.random.key(seed), 6)
    part_splits = jax.random.split(jax.random.fold_in(key_list[5], part), 6)
    return {
        "mask_tiles": jnp.clip(jax.random.uniform(part_splits[0], (TILES, TILE_PX, TILE_PX), jnp.float32, -1.0, 1.0) * level_of(part_splits[0], (TILES, TILE_PX, TILE_PX), ((0, 16),), -0.4, 0.0), -1.0, 1.0),
        "target_grid": jnp.clip(1.0 * jax.random.uniform(part_splits[1], (TILES, GRID_Y * CORE_X), jnp.float32) ** level_of(part_splits[1], (TILES, GRID_Y * CORE_X), ((0, 16),), -0.2, 0.2), 0.0, 1.0),
        "kernels": noise(key_list[2], (OWNERS, 2, KERN, FREQ_Y, FREQ_X), 8.0, 48.0, ((0, 16),), jnp.float32),
        "kern_weight": jnp.clip(jnp.exp(jax.random.uniform(key_list[3], (KERN,), jnp.float32, math.log(0.05), math.log(1.0))), 0.05, 1.0),
        "owner_list": draw_owner_list(jax.random.fold_in(jax.random.fold_in(key_list[5], part), 71), part),
    }


HIGHEST_PREC = lax.Precision.HIGHEST
RESIST_SLOPE = 3.0
RESIST_LEVEL = 1.2
DIFFUSE_RATE = 0.2
STEP_SIZE = 1.0

def phase_table(length, count):
    positions = jnp.arange(length, dtype=jnp.int32)[:, None]
    freq_ids = jnp.arange(count, dtype=jnp.int32)[None, :] - count // 2
    phase_turns = jnp.mod(positions * freq_ids, length).astype(jnp.float32) / length
    angles = 2.0 * math.pi * phase_turns
    return (jnp.cos(angles), jnp.sin(angles))

def spectra_of(windows, row_cos, row_sin, col_table):
    col_terms = jnp.einsum('npx,xb->npb', windows, col_table, precision=HIGHEST_PREC)
    half_cols = col_table.shape[1] // 2
    with_cos = col_terms[:, :, :half_cols]
    with_sin = col_terms[:, :, half_cols:]
    spec_real = jnp.einsum('pa,npb->nab', row_cos, with_cos, precision=HIGHEST_PREC) - jnp.einsum('pa,npb->nab', row_sin, with_sin, precision=HIGHEST_PREC)
    spec_imag = -(jnp.einsum('pa,npb->nab', row_sin, with_cos, precision=HIGHEST_PREC) + jnp.einsum('pa,npb->nab', row_cos, with_sin, precision=HIGHEST_PREC))
    tile_count = windows.shape[0]
    return jnp.concatenate([spec_real.reshape(tile_count, -1), spec_imag.reshape(tile_count, -1)], axis=1)

def diffuse(field):
    padded = jnp.pad(field, ((0, 0), (1, 1), (1, 1)), mode='edge')
    laplacian = padded[:, 2:, 1:-1] + padded[:, :-2, 1:-1] + padded[:, 1:-1, 2:] + padded[:, 1:-1, :-2] - 4.0 * field
    return field + DIFFUSE_RATE * laplacian

def tile_errors(spectra, targets, kern_sets, kern_weight, grid_tables):
    grid_row_cos, grid_row_sin, grid_col_cos, grid_col_sin = grid_tables
    tile_count = spectra.shape[0]
    freq_y, freq_x = (kern_sets.shape[3], kern_sets.shape[4])
    grid_y, grid_x = (grid_row_cos.shape[0], grid_col_cos.shape[0])
    spec_real = spectra[:, :freq_y * freq_x].reshape(tile_count, 1, freq_y, freq_x)
    spec_imag = spectra[:, freq_y * freq_x:].reshape(tile_count, 1, freq_y, freq_x)
    kern_real = kern_sets[:, 0]
    kern_imag = kern_sets[:, 1]
    field_real = kern_real * spec_real - kern_imag * spec_imag
    field_imag = kern_real * spec_imag + kern_imag * spec_real
    rows_real = jnp.einsum('ua,nkab->nkub', grid_row_cos, field_real, precision=HIGHEST_PREC) - jnp.einsum('ua,nkab->nkub', grid_row_sin, field_imag, precision=HIGHEST_PREC)
    rows_imag = jnp.einsum('ua,nkab->nkub', grid_row_cos, field_imag, precision=HIGHEST_PREC) + jnp.einsum('ua,nkab->nkub', grid_row_sin, field_real, precision=HIGHEST_PREC)
    amp_real = jnp.einsum('nkub,vb->nkuv', rows_real, grid_col_cos, precision=HIGHEST_PREC) - jnp.einsum('nkub,vb->nkuv', rows_imag, grid_col_sin, precision=HIGHEST_PREC)
    amp_imag = jnp.einsum('nkub,vb->nkuv', rows_real, grid_col_sin, precision=HIGHEST_PREC) + jnp.einsum('nkub,vb->nkuv', rows_imag, grid_col_cos, precision=HIGHEST_PREC)
    scale_norm = 1.0 / (64.0 * grid_y * grid_x)
    power = amp_real * amp_real + amp_imag * amp_imag
    intensity = jnp.einsum('k,nkuv->nuv', kern_weight, power, precision=HIGHEST_PREC) * (scale_norm * scale_norm)
    blurred = intensity
    for rounds in range(DIFF_STEPS):
        blurred = diffuse(blurred)
    resist = jax.nn.sigmoid(RESIST_SLOPE * (blurred - RESIST_LEVEL))
    core_cols = targets.shape[1] // grid_y
    offset = (grid_x - core_cols) // 2
    inner_cols = resist[:, :, offset:offset + core_cols]
    misfit = inner_cols - targets.reshape(tile_count, grid_y, core_cols)
    return lax.optimization_barrier(jnp.sum(misfit * misfit, axis=(1, 2)))

def window_stack(current):
    zero_cols = jnp.zeros((1, TILE_PX, AMBIT), current.dtype)
    left_parts = jnp.concatenate([zero_cols, current[:-1, :, TILE_PX - AMBIT:]], axis=0)
    right_parts = jnp.concatenate([current[1:, :, :AMBIT], zero_cols], axis=0)
    return jnp.concatenate([left_parts, current, right_parts], axis=2)

def reference(mask_tiles, target_grid, kernels, kern_weight, owner_list):
    row_cos, row_sin = phase_table(TILE_PX, FREQ_Y)
    col_cos, col_sin = phase_table(WIN, FREQ_X)
    col_table = jnp.concatenate([col_cos, col_sin], axis=1)
    grid_tables = phase_table(GRID_Y, FREQ_Y) + phase_table(GRID_X, FREQ_X)
    owner_column = owner_list[:, 0].astype(jnp.int32)

    def one_tile(tile_items):
        spectra_row, target_row, owner_id = tile_items
        kern_set = lax.dynamic_index_in_dim(kernels, owner_id, 0, keepdims=True)
        return tile_errors(spectra_row[None], target_row[None], kern_set, kern_weight, grid_tables)[0]

    def total_error(current):
        spectra = spectra_of(window_stack(current), row_cos, row_sin, col_table)
        errors = lax.map(one_tile, (spectra, target_grid, owner_column))
        return (jnp.sum(errors), errors)
    current = mask_tiles
    errors = None
    for rounds in range(ITERS):
        total_err, pullback, errors = jax.vjp(total_error, current, has_aux=True)
        gradient = pullback(jnp.ones_like(total_err))[0]
        current = current - STEP_SIZE * gradient
    owner_ids = jnp.arange(OWNERS, dtype=jnp.int32)[:, None]
    onehot = (owner_column[None, :] == owner_ids).astype(jnp.float32)
    owner_error = jnp.dot(onehot, errors, precision=HIGHEST_PREC) / (GRID_Y * CORE_X)
    return (current, owner_error)
```

```python
import functools

import jax
import jax.numpy as jnp
import ml_dtypes
import numpy as np
from jax import lax
from jax.experimental import pallas as pl
from jax.experimental.pallas import tpu as pltpu
from jax.sharding import PartitionSpec as P

AMBIT = 256
DIFF_STEPS = 2
GRID_X = 192
GRID_Y = 128
CORE_X = 128
MOST = 2
ROWS = 80
LANES = 128

RESIST_SLOPE = 3.0
RESIST_LEVEL = 1.2
DIFFUSE_RATE = 0.2
STEP_SIZE = 1.0

F32 = jnp.float32
BF16 = jnp.bfloat16
HIGHEST = lax.Precision.HIGHEST


def angle(length, positions, freqs):
    turns = np.mod(np.outer(positions, freqs), length).astype(np.float64) / length
    return 2.0 * np.pi * turns


def halves(table):
    high = table.astype(np.float32).astype(ml_dtypes.bfloat16)
    low = (table - high.astype(np.float64)).astype(np.float32).astype(ml_dtypes.bfloat16)
    return high, low


def real_basis(length, count):
    half = count // 2
    return np.concatenate(
        [
            np.cos(angle(length, np.arange(length), np.arange(half + 1))),
            np.sin(angle(length, np.arange(length), np.arange(1, half + 1))),
        ],
        axis=1,
    )


def pickers(count, padded_freqs, padded_basis):
    half = count // 2
    cos_pick = np.zeros((padded_freqs, padded_basis), np.float32)
    sin_pick = np.zeros((padded_freqs, padded_basis), np.float32)
    for place in range(count):
        freq = place - half
        cos_pick[place, abs(freq)] = 1.0
        if freq:
            sin_pick[place, half + abs(freq)] = np.sign(freq)
    return cos_pick, sin_pick


def split(x):
    high = x.astype(BF16)
    low = (x - high.astype(F32)).astype(BF16)
    return high, low


def nn(a, b):
    return lax.dot_general(a, b, (((1,), (0,)), ((), ())), preferred_element_type=F32)


def nt(a, b):
    return lax.dot_general(a, b, (((1,), (1,)), ((), ())), preferred_element_type=F32)


def tn(a, b):
    return lax.dot_general(a, b, (((0,), (0,)), ((), ())), preferred_element_type=F32)


def nn3(a, b_high, b_low):
    a_high, a_low = split(a)
    return nn(a_high, b_high) + (nn(a_high, b_low) + nn(a_low, b_high))


def exact(dot, a, b):
    return lax.dot_general(a, b, dot, precision=HIGHEST, preferred_element_type=F32)


NN = (((1,), (0,)), ((), ()))
TN = (((0,), (0,)), ((), ()))
NT = (((1,), (1,)), ((), ()))


def coeffs_kernel(mask_ref, row_ref, col_ref, out_ref, total):
    step = pl.program_id(0)

    @pl.when(step == 0)
    def _():
        total[...] = jnp.zeros_like(total)

    m_high, m_low = split(mask_ref[0])
    both = nn(row_ref[...], m_high)
    total[...] += both[:ROWS] + (both[ROWS:] + nn(row_ref[:ROWS, :], m_low))

    @pl.when(step == pl.num_programs(0) - 1)
    def _():
        r_high, r_low = split(total[...])
        res = nn(r_high, col_ref[0]) + (nn(r_high, col_ref[1]) + nn(r_low, col_ref[0]))
        for piece in range(3):
            out_ref[piece] = res[:72, piece * LANES : (piece + 1) * LANES]


def update_kernel(mask_ref, slope_ref, row_ref, col_ref, out_ref, q_ref):
    @pl.when(pl.program_id(0) == 0)
    def _():
        d = jnp.concatenate([slope_ref[0], slope_ref[1], slope_ref[2]], axis=1)
        d = jnp.concatenate([d, jnp.zeros((ROWS - 72, 3 * LANES), F32)], axis=0)
        d_high, d_low = split(d)
        q = nt(d_high, col_ref[0]) + (nt(d_high, col_ref[1]) + nt(d_low, col_ref[0]))
        q_high, q_low = split(q)
        q_ref[:ROWS] = q_high
        q_ref[ROWS : 2 * ROWS] = q_high
        q_ref[2 * ROWS :] = q_low

    out_ref[0] = mask_ref[0] - STEP_SIZE * nn(row_ref[...], q_ref[...])


def diffuse(x):
    v_len, u_len = x.shape
    up = jnp.concatenate([x[:1], x[:-1]], axis=0)
    down = jnp.concatenate([x[1:], x[-1:]], axis=0)
    left = jnp.concatenate([x[:, :1], x[:, :-1]], axis=1)
    right = jnp.concatenate([x[:, 1:], x[:, -1:]], axis=1)
    return x + DIFFUSE_RATE * (up + down + left + right - 4.0 * x)


def owner_kernel(
    ids_ref, live_ref, weight_ref, coeff_ref, target_ref, kern_ref, py_ref, px_ref, cs_ref, wy_ref,
    slope_ref, err_ref, amps, s_ref, ds_ref, intensity,
):
    slot = pl.program_id(0)
    freq_y, freq_x = kern_ref.shape[2], kern_ref.shape[3]
    kern = kern_ref.shape[1]

    def kern_pair(k):
        pad = jnp.zeros((freq_y, LANES - freq_x), F32)
        return (
            jnp.concatenate([kern_ref[0, k], pad], axis=1),
            jnp.concatenate([kern_ref[1, k], pad], axis=1),
        )

    @pl.when(live_ref[slot] == 0)
    def _():
        slope_ref[...] = jnp.zeros_like(slope_ref)

    @pl.when(slot == 0)
    def _():
        err_ref[...] = jnp.zeros_like(err_ref)

    @pl.when(live_ref[slot] != 0)
    def _():
        u = exact(NN, py_ref[...], coeff_ref[0])
        u_cos, u_sin = u[:freq_y], u[freq_y:]
        px_cos, px_sin = px_ref[0], px_ref[1]
        s_ref[0] = exact(NT, u_cos, px_cos) - exact(NT, u_sin, px_sin)
        s_ref[1] = -(exact(NT, u_sin, px_cos) + exact(NT, u_cos, px_sin))
        intensity[...] = jnp.zeros_like(intensity)

        def forward(pair, carry):
            spec_re, spec_im = s_ref[0], s_ref[1]
            rows = []
            for j in range(2):
                h_re, h_im = kern_pair(2 * pair + j)
                f_re = h_re * spec_re - h_im * spec_im
                f_im = h_re * spec_im + h_im * spec_re
                rows.append(jnp.concatenate([f_re, -f_im], axis=1))
                rows.append(jnp.concatenate([f_im, f_re], axis=1))
            f_high, f_low = split(jnp.concatenate(rows, axis=0))
            both = nt(cs_ref[...], f_high)
            x = both[:GRID_X] + (both[GRID_X:] + nt(cs_ref[:GRID_X, :], f_low))
            x_high, x_low = split(x)
            for j in range(2):
                k = 2 * pair + j
                part = slice(j * LANES, (j + 1) * LANES)
                xh, xl = x_high[:, part], x_low[:, part]
                amp = nn(jnp.concatenate([xh, xl, xh], axis=1), wy_ref[...])
                amps[k] = amp
                re, im = amp[:, :LANES], amp[:, LANES:]
                intensity[...] += weight_ref[k] * (re * re + im * im)
            return carry

        lax.fori_loop(0, kern // 2, forward, 0)
        blurred = intensity[...]
        for _ in range(DIFF_STEPS):
            blurred = diffuse(blurred)
        resist = 1.0 / (1.0 + jnp.exp(-RESIST_SLOPE * (blurred - RESIST_LEVEL)))
        offset = (GRID_X - CORE_X) // 2
        inner = resist[offset : offset + CORE_X]
        misfit = inner - target_ref[0].T
        err_ref[...] += jnp.sum(misfit * misfit, keepdims=True)
        core = (2.0 * RESIST_SLOPE) * misfit * inner * (1.0 - inner)
        edge = jnp.zeros((offset, GRID_Y), F32)
        slope = jnp.concatenate([edge, core, edge], axis=0)
        for _ in range(DIFF_STEPS):
            slope = diffuse(slope)
        intensity[...] = 2.0 * slope
        ds_ref[...] = jnp.zeros_like(ds_ref)

        def backward(k, carry):
            gain = weight_ref[k] * intensity[...]
            amp = amps[k]
            d = jnp.concatenate([gain * amp[:, :LANES], gain * amp[:, LANES:]], axis=1)
            d_high, d_low = split(d)
            w_high = wy_ref[:LANES]
            w_low = wy_ref[2 * LANES :]
            dx = nt(w_high, d_high) + (nt(w_low, d_high) + nt(w_high, d_low))
            x_high, x_low = split(dx)
            c_high, c_low = cs_ref[:GRID_X, :], cs_ref[GRID_X:, :]
            df = nn(x_high, c_high) + (nn(x_high, c_low) + nn(x_low, c_high))
            d_re, d_im = df[:freq_y], df[freq_y:]
            f_re = d_re[:, :LANES] + d_im[:, LANES:]
            f_im = d_im[:, :LANES] - d_re[:, LANES:]
            h_re, h_im = kern_pair(k)
            ds_ref[0] += h_re * f_re + h_im * f_im
            ds_ref[1] += h_re * f_im - h_im * f_re
            return carry

        lax.fori_loop(0, kern, backward, 0)
        ds_re, ds_im = ds_ref[0], ds_ref[1]
        du_cos = exact(NN, ds_re, px_cos) - exact(NN, ds_im, px_sin)
        du_sin = -(exact(NN, ds_re, px_sin) + exact(NN, ds_im, px_cos))
        slope_ref[0] = exact(TN, py_ref[...], jnp.concatenate([du_cos, du_sin], axis=0))


def tables(tile_px, freq_y, freq_x):
    win = tile_px + 2 * AMBIT
    row = np.zeros((tile_px, ROWS))
    row[:, : freq_y + 1] = real_basis(tile_px, freq_y)
    col = np.zeros((win, LANES))
    col[:, : freq_x + 1] = real_basis(win, freq_x)
    pieces = np.zeros((tile_px, 3 * LANES))
    pieces[:, :LANES] = col[AMBIT : AMBIT + tile_px]
    pieces[tile_px - AMBIT :, LANES : 2 * LANES] = col[:AMBIT]
    pieces[:AMBIT, 2 * LANES :] = col[AMBIT + tile_px :]
    r_high, r_low = halves(row)
    row_fwd = np.concatenate([r_high.T, r_low.T], axis=0)
    row_bwd = np.concatenate([r_high, r_low, r_high], axis=1)
    col_tab = np.stack(halves(pieces))
    py = np.concatenate(pickers(freq_y, freq_y, 72), axis=0)
    px = np.stack(pickers(freq_x, LANES, LANES))
    ax = angle(GRID_X, np.arange(GRID_X), np.arange(freq_x) - freq_x // 2)
    cs = np.zeros((GRID_X, 2 * LANES))
    cs[:, :freq_x] = np.cos(ax)
    cs[:, LANES : LANES + freq_x] = np.sin(ax)
    cs = np.concatenate(halves(cs), axis=0)
    ay = angle(GRID_Y, np.arange(freq_y) - freq_y // 2, np.arange(GRID_Y))
    wy = np.block([[np.cos(ay), np.sin(ay)], [-np.sin(ay), np.cos(ay)]]) / (64.0 * GRID_Y * GRID_X)
    w_high, w_low = halves(wy)
    wy = np.concatenate([w_high, w_high, w_low], axis=0)
    return row_fwd, row_bwd, col_tab, py, px, cs, wy


def whole(shape, memory_space=None):
    return pl.BlockSpec(shape, lambda *_: (0,) * len(shape))


def on_device(mask_tiles, target_grid, kernels, kern_weight, owner_list):
    tile_px = mask_tiles.shape[1]
    kern, freq_y, freq_x = kernels.shape[2:]
    count = lax.axis_size("tile")
    row_fwd, row_bwd, col_tab, py, px, cs, wy = tables(tile_px, freq_y, freq_x)
    me = lax.axis_index("tile")

    mine = owner_list[:, 0] == me
    places = jnp.arange(count, dtype=jnp.int32)
    first = jnp.min(jnp.where(mine, places, count))
    last = jnp.max(jnp.where(mine, places, -1))
    ids = jnp.stack([jnp.minimum(first, count - 1), jnp.maximum(last, 0)])
    live = jnp.stack([first < count, last > first]).astype(jnp.int32)

    targets = lax.all_gather(target_grid.reshape(GRID_Y, CORE_X), "tile", axis=0)

    chunk = 256
    steps = tile_px // chunk
    pieces = pl.pallas_call(
        coeffs_kernel,
        grid=(steps,),
        in_specs=[
            pl.BlockSpec((1, chunk, tile_px), lambda i: (0, i, 0)),
            pl.BlockSpec((2 * ROWS, chunk), lambda i: (0, i)),
            whole(col_tab.shape),
        ],
        out_specs=whole((3, 72, LANES)),
        out_shape=jax.ShapeDtypeStruct((3, 72, LANES), F32),
        scratch_shapes=[pltpu.VMEM((ROWS, tile_px), F32)],
        compiler_params=pltpu.CompilerParams(vmem_limit_bytes=40 << 20),
        name="coeffs",
    )(mask_tiles, row_fwd, col_tab)

    ring = [(i, i + 1) for i in range(count - 1)]
    from_left = lax.ppermute(pieces[1], "tile", ring)
    from_right = lax.ppermute(pieces[2], "tile", [(b, a) for a, b in ring])
    coeffs = lax.all_gather(pieces[0] + from_left + from_right, "tile", axis=0)

    slopes, errors = pl.pallas_call(
        owner_kernel,
        grid_spec=pltpu.PrefetchScalarGridSpec(
            num_scalar_prefetch=3,
            grid=(MOST,),
            in_specs=[
                pl.BlockSpec((1, 72, LANES), lambda s, ids, live, w: (ids[s], 0, 0)),
                pl.BlockSpec((1, GRID_Y, CORE_X), lambda s, ids, live, w: (ids[s], 0, 0)),
                whole((2, kern, freq_y, freq_x)),
                whole(py.shape),
                whole(px.shape),
                whole(cs.shape),
                whole(wy.shape),
            ],
            out_specs=[
                pl.BlockSpec((1, 72, LANES), lambda s, *_: (s, 0, 0)),
                whole((1, 1)),
            ],
            scratch_shapes=[
                pltpu.VMEM((kern, GRID_X, 2 * GRID_Y), F32),
                pltpu.VMEM((2, freq_y, LANES), F32),
                pltpu.VMEM((2, freq_y, LANES), F32),
                pltpu.VMEM((GRID_X, GRID_Y), F32),
            ],
        ),
        out_shape=[
            jax.ShapeDtypeStruct((MOST, 72, LANES), F32),
            jax.ShapeDtypeStruct((1, 1), F32),
        ],
        compiler_params=pltpu.CompilerParams(vmem_limit_bytes=40 << 20),
        name="owner",
    )(ids, live, kern_weight, coeffs, targets, kernels[0], py, px, cs, wy)

    gathered = lax.all_gather(slopes, "tile", axis=0)
    owners = owner_list[:, 0]
    same = owners[:, None] == owners[None, :]
    rank = jnp.sum(same & (places[None, :] < places[:, None]), axis=1).astype(jnp.int32)

    def slope_of(tile):
        inside = jnp.clip(tile, 0, count - 1)
        flat = gathered.reshape(count * MOST, 72, LANES)
        place = owners[inside] * MOST + rank[inside]
        found = lax.dynamic_index_in_dim(flat, place, 0, keepdims=False)
        return jnp.where(inside == tile, found, 0.0)

    my_slopes = jnp.stack([slope_of(me), slope_of(me + 1), slope_of(me - 1)])
    out = pl.pallas_call(
        update_kernel,
        grid=(steps,),
        in_specs=[
            pl.BlockSpec((1, chunk, tile_px), lambda i: (0, i, 0)),
            whole((3, 72, LANES)),
            pl.BlockSpec((chunk, 3 * ROWS), lambda i: (i, 0)),
            whole(col_tab.shape),
        ],
        out_specs=pl.BlockSpec((1, chunk, tile_px), lambda i: (0, i, 0)),
        out_shape=jax.ShapeDtypeStruct(mask_tiles.shape, F32),
        scratch_shapes=[pltpu.VMEM((3 * ROWS, tile_px), BF16)],
        compiler_params=pltpu.CompilerParams(vmem_limit_bytes=40 << 20),
        name="update",
    )(mask_tiles, my_slopes, row_bwd, col_tab)
    return out, (errors / (GRID_Y * CORE_X)).reshape(1)


def solution(mesh):
    placed = (
        P(("stripe", "tile"), None, None),
        P(("stripe", "tile"), None),
        P("tile", None, None, None, None),
        P(),
        P("stripe", None),
    )
    return jax.shard_map(
        on_device,
        mesh=mesh,
        in_specs=placed,
        out_specs=(P(("stripe", "tile"), None, None), P(("stripe", "tile"))),
        check_vma=False,
    )
```

```python
import functools

import jax
import jax.numpy as jnp
import ml_dtypes
import numpy as np
from jax import lax
from jax.experimental import pallas as pl
from jax.experimental.pallas import tpu as pltpu
from jax.sharding import PartitionSpec as P

AMBIT = 256
DIFF_STEPS = 2
GRID_X = 192
GRID_Y = 128
CORE_X = 128
MOST = 2
ROWS = 80
LANES = 128
VMEM_BYTES = 60 << 20

RESIST_SLOPE = 3.0
RESIST_LEVEL = 1.2
DIFFUSE_RATE = 0.2
STEP_SIZE = 1.0

F32 = jnp.float32
BF16 = jnp.bfloat16
HIGHEST = lax.Precision.HIGHEST


def angle(length, positions, freqs):
    turns = np.mod(np.outer(positions, freqs), length).astype(np.float64) / length
    return 2.0 * np.pi * turns


def halves(table):
    high = table.astype(np.float32).astype(ml_dtypes.bfloat16)
    low = (table - high.astype(np.float64)).astype(np.float32).astype(ml_dtypes.bfloat16)
    return high, low


def real_basis(length, count):
    half = count // 2
    return np.concatenate(
        [
            np.cos(angle(length, np.arange(length), np.arange(half + 1))),
            np.sin(angle(length, np.arange(length), np.arange(1, half + 1))),
        ],
        axis=1,
    )


def pickers(count, padded_freqs, padded_basis):
    half = count // 2
    cos_pick = np.zeros((padded_freqs, padded_basis), np.float32)
    sin_pick = np.zeros((padded_freqs, padded_basis), np.float32)
    for place in range(count):
        freq = place - half
        cos_pick[place, abs(freq)] = 1.0
        if freq:
            sin_pick[place, half + abs(freq)] = np.sign(freq)
    return cos_pick, sin_pick


def split(x):
    high = x.astype(BF16)
    low = (x - high.astype(F32)).astype(BF16)
    return high, low


def nn(a, b):
    return lax.dot_general(a, b, (((1,), (0,)), ((), ())), preferred_element_type=F32)


def nt(a, b):
    return lax.dot_general(a, b, (((1,), (1,)), ((), ())), preferred_element_type=F32)


def tn(a, b):
    return lax.dot_general(a, b, (((0,), (0,)), ((), ())), preferred_element_type=F32)


def nn3(a, b_high, b_low):
    a_high, a_low = split(a)
    return nn(a_high, b_high) + (nn(a_high, b_low) + nn(a_low, b_high))


def exact(dot, a, b):
    return lax.dot_general(a, b, dot, precision=HIGHEST, preferred_element_type=F32)


NN = (((1,), (0,)), ((), ()))
TN = (((0,), (0,)), ((), ()))
NT = (((1,), (1,)), ((), ()))


def coeffs_kernel(mask_ref, row_ref, col_ref, out_ref, total):
    step = pl.program_id(0)

    @pl.when(step == 0)
    def _():
        total[...] = jnp.zeros_like(total)

    m_high, m_low = split(mask_ref[0])
    both = nn(row_ref[...], m_high)
    total[...] += both[:ROWS] + (both[ROWS:] + nn(row_ref[:ROWS, :], m_low))

    @pl.when(step == pl.num_programs(0) - 1)
    def _():
        r_high, r_low = split(total[...])
        res = nn(r_high, col_ref[0]) + (nn(r_high, col_ref[1]) + nn(r_low, col_ref[0]))
        for piece in range(3):
            out_ref[piece] = res[:72, piece * LANES : (piece + 1) * LANES]


def update_kernel(mask_ref, slope_ref, row_ref, col_ref, out_ref, q_ref):
    @pl.when(pl.program_id(0) == 0)
    def _():
        d = jnp.concatenate([slope_ref[0], slope_ref[1], slope_ref[2]], axis=1)
        d = jnp.concatenate([d, jnp.zeros((ROWS - 72, 3 * LANES), F32)], axis=0)
        d_high, d_low = split(d)
        q = nt(d_high, col_ref[0]) + (nt(d_high, col_ref[1]) + nt(d_low, col_ref[0]))
        q_high, q_low = split(q)
        q_ref[:ROWS] = q_high
        q_ref[ROWS : 2 * ROWS] = q_high
        q_ref[2 * ROWS :] = q_low

    out_ref[0] = mask_ref[0] - STEP_SIZE * nn(row_ref[...], q_ref[...])


def diffuse(x):
    v_len, u_len = x.shape
    up = jnp.concatenate([x[:1], x[:-1]], axis=0)
    down = jnp.concatenate([x[1:], x[-1:]], axis=0)
    left = jnp.concatenate([x[:, :1], x[:, :-1]], axis=1)
    right = jnp.concatenate([x[:, 1:], x[:, -1:]], axis=1)
    return x + DIFFUSE_RATE * (up + down + left + right - 4.0 * x)


def owner_kernel(
    ids_ref, live_ref, weight_ref, coeff_ref, target_ref, kern_ref, py_ref, px_ref, cs_ref, wy_ref,
    slope_ref, err_ref, amps, s_ref, ds_ref, intensity,
):
    slot = pl.program_id(0)
    freq_y, freq_x = kern_ref.shape[2], kern_ref.shape[3]
    kern = kern_ref.shape[1]

    def kern_pair(k):
        pad = jnp.zeros((freq_y, LANES - freq_x), F32)
        return (
            jnp.concatenate([kern_ref[0, k], pad], axis=1),
            jnp.concatenate([kern_ref[1, k], pad], axis=1),
        )

    @pl.when(live_ref[slot] == 0)
    def _():
        slope_ref[...] = jnp.zeros_like(slope_ref)

    @pl.when(slot == 0)
    def _():
        err_ref[...] = jnp.zeros_like(err_ref)

    @pl.when(live_ref[slot] != 0)
    def _():
        u = exact(NN, py_ref[...], coeff_ref[0])
        u_cos, u_sin = u[:freq_y], u[freq_y:]
        px_cos, px_sin = px_ref[0], px_ref[1]
        s_ref[0] = exact(NT, u_cos, px_cos) - exact(NT, u_sin, px_sin)
        s_ref[1] = -(exact(NT, u_sin, px_cos) + exact(NT, u_cos, px_sin))
        intensity[...] = jnp.zeros_like(intensity)

        def forward(pair, carry):
            spec_re, spec_im = s_ref[0], s_ref[1]
            rows = []
            for j in range(2):
                h_re, h_im = kern_pair(2 * pair + j)
                f_re = h_re * spec_re - h_im * spec_im
                f_im = h_re * spec_im + h_im * spec_re
                rows.append(jnp.concatenate([f_re, -f_im], axis=1))
                rows.append(jnp.concatenate([f_im, f_re], axis=1))
            f_high, f_low = split(jnp.concatenate(rows, axis=0))
            both = nt(cs_ref[...], f_high)
            x = both[:GRID_X] + (both[GRID_X:] + nt(cs_ref[:GRID_X, :], f_low))
            x_high, x_low = split(x)
            for j in range(2):
                k = 2 * pair + j
                part = slice(j * LANES, (j + 1) * LANES)
                xh, xl = x_high[:, part], x_low[:, part]
                amp = nn(jnp.concatenate([xh, xl, xh], axis=1), wy_ref[...])
                amps[k] = amp
                re, im = amp[:, :LANES], amp[:, LANES:]
                intensity[...] += weight_ref[k] * (re * re + im * im)
            return carry

        lax.fori_loop(0, kern // 2, forward, 0)
        blurred = intensity[...]
        for _ in range(DIFF_STEPS):
            blurred = diffuse(blurred)
        resist = 1.0 / (1.0 + jnp.exp(-RESIST_SLOPE * (blurred - RESIST_LEVEL)))
        offset = (GRID_X - CORE_X) // 2
        inner = resist[offset : offset + CORE_X]
        misfit = inner - target_ref[0].T
        err_ref[...] += jnp.sum(misfit * misfit, keepdims=True)
        core = (2.0 * RESIST_SLOPE) * misfit * inner * (1.0 - inner)
        edge = jnp.zeros((offset, GRID_Y), F32)
        slope = jnp.concatenate([edge, core, edge], axis=0)
        for _ in range(DIFF_STEPS):
            slope = diffuse(slope)
        intensity[...] = 2.0 * slope
        ds_ref[...] = jnp.zeros_like(ds_ref)

        def backward(k, carry):
            gain = weight_ref[k] * intensity[...]
            amp = amps[k]
            d = jnp.concatenate([gain * amp[:, :LANES], gain * amp[:, LANES:]], axis=1)
            d_high, d_low = split(d)
            w_high = wy_ref[:LANES]
            w_low = wy_ref[2 * LANES :]
            dx = nt(w_high, d_high) + (nt(w_low, d_high) + nt(w_high, d_low))
            x_high, x_low = split(dx)
            c_high, c_low = cs_ref[:GRID_X, :], cs_ref[GRID_X:, :]
            df = nn(x_high, c_high) + (nn(x_high, c_low) + nn(x_low, c_high))
            d_re, d_im = df[:freq_y], df[freq_y:]
            f_re = d_re[:, :LANES] + d_im[:, LANES:]
            f_im = d_im[:, :LANES] - d_re[:, LANES:]
            h_re, h_im = kern_pair(k)
            ds_ref[0] += h_re * f_re + h_im * f_im
            ds_ref[1] += h_re * f_im - h_im * f_re
            return carry

        lax.fori_loop(0, kern, backward, 0)
        ds_re, ds_im = ds_ref[0], ds_ref[1]
        du_cos = exact(NN, ds_re, px_cos) - exact(NN, ds_im, px_sin)
        du_sin = -(exact(NN, ds_re, px_sin) + exact(NN, ds_im, px_cos))
        slope_ref[0] = exact(TN, py_ref[...], jnp.concatenate([du_cos, du_sin], axis=0))


def factors(count):
    pair = 2 if count % 2 == 0 else 1
    rest = count // pair
    inner = max(d for d in range(1, rest + 1) if rest % d == 0 and d * d <= rest)
    return rest // inner, inner, pair


def wrapped(index, size):
    return lax.rem(index + size, size)


class Place:
    def __init__(self, count):
        self.count = count
        self.outer, self.inner, self.pair = factors(count)
        self.me = lax.axis_index("tile")
        self.c = lax.rem(self.me, self.pair)
        self.b = lax.rem(self.me // self.pair, self.inner)
        self.a = self.me // (self.pair * self.inner)

    def at(self, da, db, dc):
        a = wrapped(self.a + da, self.outer)
        b = wrapped(self.b + db, self.inner)
        c = wrapped(self.c + dc, self.pair)
        return (a * self.inner + b) * self.pair + c

    def partners(self):
        return (
            [self.at(d, 0, 0) for d in range(1, self.outer)]
            + [self.at(0, d, 0) for d in range(1, self.inner)]
            + [self.at(0, 0, d) for d in range(1, self.pair)]
        )


def meet(devices):
    barrier = pltpu.get_barrier_semaphore()
    for device in devices:
        pl.semaphore_signal(
            barrier, inc=1, device_id={"tile": device}, device_id_type=pl.DeviceIdType.MESH
        )
    pl.semaphore_wait(barrier, len(devices))


class Gather:
    def __init__(self, place, slots, send, recv):
        self.place, self.slots, self.send, self.recv = place, slots, send, recv
        self.started = []

    def copy(self, slot, device, index):
        return pltpu.make_async_remote_copy(
            src_ref=self.slots.at[slot],
            dst_ref=self.slots.at[slot],
            send_sem=self.send.at[index],
            recv_sem=self.recv.at[slot],
            device_id={"tile": device},
            device_id_type=pl.DeviceIdType.MESH,
        )

    def push(self, slot, device):
        copy = self.copy(slot, device, len(self.started))
        copy.start()
        self.started.append(copy)

    def arrive(self, slot):
        self.copy(slot, self.place.at(1, 0, 0), 0).wait_recv()

    def to_pair(self, slot):
        for d in range(1, self.place.pair):
            self.push(slot, self.place.at(0, 0, d))

    def to_inner(self, slot):
        for d in range(1, self.place.inner):
            self.push(slot, self.place.at(0, d, 0))

    def own(self):
        p = self.place
        for d in range(1, p.outer):
            self.push(p.me, p.at(d, 0, 0))
        self.to_inner(p.me)
        self.to_pair(p.me)

    def outer_arrivals(self):
        for d in range(1, self.place.outer):
            slot = self.place.at(-d, 0, 0)
            self.arrive(slot)
            self.to_inner(slot)
            self.to_pair(slot)

    def inner_arrivals(self):
        for d in range(self.place.outer):
            for e in range(1, self.place.inner):
                slot = self.place.at(-d, -e, 0)
                self.arrive(slot)
                self.to_pair(slot)

    def finish(self):
        p = self.place
        for d in range(p.outer):
            for e in range(p.inner):
                for f in range(1, p.pair):
                    self.arrive(p.at(-d, -e, -f))
        for copy in self.started:
            copy.wait_send()


def spread_kernel(
    count, piece_ref, target_ref, coeff_ref, all_target_ref, near, near_send, near_recv,
    send_c, recv_c, send_t, recv_t,
):
    place = Place(count)
    me = place.me
    right, left = wrapped(me + 1, count), wrapped(me - 1, count)
    coeff = Gather(place, coeff_ref, send_c, recv_c)
    target = Gather(place, all_target_ref, send_t, recv_t)
    all_target_ref[me] = target_ref[...]
    meet([right, left] + place.partners())
    sides = []
    for side, device in ((0, right), (1, left)):
        copy = pltpu.make_async_remote_copy(
            src_ref=piece_ref.at[1 + side],
            dst_ref=near.at[side],
            send_sem=near_send.at[side],
            recv_sem=near_recv.at[side],
            device_id={"tile": device},
            device_id_type=pl.DeviceIdType.MESH,
        )
        copy.start()
        sides.append(copy)
    target.own()
    for copy in sides:
        copy.wait()
    own = piece_ref[0]
    own = own + jnp.where(me > 0, near[0], 0.0)
    own = own + jnp.where(me < count - 1, near[1], 0.0)
    coeff_ref[me] = own
    coeff.own()
    target.outer_arrivals()
    coeff.outer_arrivals()
    target.inner_arrivals()
    coeff.inner_arrivals()
    target.finish()
    coeff.finish()


def collect_kernel(count, slope_ref, all_ref, send, recv):
    place = Place(count)
    gather = Gather(place, all_ref, send, recv)
    all_ref[place.me] = slope_ref[...]
    meet(place.partners())
    gather.own()
    gather.outer_arrivals()
    gather.inner_arrivals()
    gather.finish()


def tables(tile_px, freq_y, freq_x):
    win = tile_px + 2 * AMBIT
    row = np.zeros((tile_px, ROWS))
    row[:, : freq_y + 1] = real_basis(tile_px, freq_y)
    col = np.zeros((win, LANES))
    col[:, : freq_x + 1] = real_basis(win, freq_x)
    pieces = np.zeros((tile_px, 3 * LANES))
    pieces[:, :LANES] = col[AMBIT : AMBIT + tile_px]
    pieces[tile_px - AMBIT :, LANES : 2 * LANES] = col[:AMBIT]
    pieces[:AMBIT, 2 * LANES :] = col[AMBIT + tile_px :]
    r_high, r_low = halves(row)
    row_fwd = np.concatenate([r_high.T, r_low.T], axis=0)
    row_bwd = np.concatenate([r_high, r_low, r_high], axis=1)
    col_tab = np.stack(halves(pieces))
    py = np.concatenate(pickers(freq_y, freq_y, 72), axis=0)
    px = np.stack(pickers(freq_x, LANES, LANES))
    ax = angle(GRID_X, np.arange(GRID_X), np.arange(freq_x) - freq_x // 2)
    cs = np.zeros((GRID_X, 2 * LANES))
    cs[:, :freq_x] = np.cos(ax)
    cs[:, LANES : LANES + freq_x] = np.sin(ax)
    cs = np.concatenate(halves(cs), axis=0)
    ay = angle(GRID_Y, np.arange(freq_y) - freq_y // 2, np.arange(GRID_Y))
    wy = np.block([[np.cos(ay), np.sin(ay)], [-np.sin(ay), np.cos(ay)]]) / (64.0 * GRID_Y * GRID_X)
    w_high, w_low = halves(wy)
    wy = np.concatenate([w_high, w_high, w_low], axis=0)
    return row_fwd, row_bwd, col_tab, py, px, cs, wy


def whole(shape, memory_space=None):
    return pl.BlockSpec(shape, lambda *_: (0,) * len(shape))


def on_device(mask_tiles, target_grid, kernels, kern_weight, owner_list):
    tile_px = mask_tiles.shape[1]
    kern, freq_y, freq_x = kernels.shape[2:]
    count = lax.axis_size("tile")
    row_fwd, row_bwd, col_tab, py, px, cs, wy = tables(tile_px, freq_y, freq_x)
    me = lax.axis_index("tile")

    mine = owner_list[:, 0] == me
    places = jnp.arange(count, dtype=jnp.int32)
    first = jnp.min(jnp.where(mine, places, count))
    last = jnp.max(jnp.where(mine, places, -1))
    ids = jnp.stack([jnp.minimum(first, count - 1), jnp.maximum(last, 0)])
    live = jnp.stack([first < count, last > first]).astype(jnp.int32)

    chunk = 256
    steps = tile_px // chunk
    pieces = pl.pallas_call(
        coeffs_kernel,
        grid=(steps,),
        in_specs=[
            pl.BlockSpec((1, chunk, tile_px), lambda i: (0, i, 0)),
            pl.BlockSpec((2 * ROWS, chunk), lambda i: (0, i)),
            whole(col_tab.shape),
        ],
        out_specs=whole((3, 72, LANES)),
        out_shape=jax.ShapeDtypeStruct((3, 72, LANES), F32),
        scratch_shapes=[pltpu.VMEM((ROWS, tile_px), F32)],
        compiler_params=pltpu.CompilerParams(vmem_limit_bytes=VMEM_BYTES),
        name="coeffs",
    )(mask_tiles, row_fwd, col_tab)

    vmem = pl.BlockSpec(memory_space=pltpu.VMEM)
    dma = pltpu.SemaphoreType.DMA
    coeffs, targets = pl.pallas_call(
        functools.partial(spread_kernel, count),
        in_specs=[vmem, vmem],
        out_specs=[vmem, vmem],
        out_shape=[
            jax.ShapeDtypeStruct((count, 72, LANES), F32),
            jax.ShapeDtypeStruct((count, GRID_Y, CORE_X), F32),
        ],
        scratch_shapes=[pltpu.VMEM((2, 72, LANES), F32), dma((2,)), dma((2,))]
        + [dma((count,))] * 4,
        compiler_params=pltpu.CompilerParams(
            collective_id=0, has_side_effects=True, vmem_limit_bytes=VMEM_BYTES
        ),
        name="spread",
    )(pieces, target_grid.reshape(GRID_Y, CORE_X))

    slopes, errors = pl.pallas_call(
        owner_kernel,
        grid_spec=pltpu.PrefetchScalarGridSpec(
            num_scalar_prefetch=3,
            grid=(MOST,),
            in_specs=[
                pl.BlockSpec((1, 72, LANES), lambda s, ids, live, w: (ids[s], 0, 0)),
                pl.BlockSpec((1, GRID_Y, CORE_X), lambda s, ids, live, w: (ids[s], 0, 0)),
                whole((2, kern, freq_y, freq_x)),
                whole(py.shape),
                whole(px.shape),
                whole(cs.shape),
                whole(wy.shape),
            ],
            out_specs=[
                pl.BlockSpec((1, 72, LANES), lambda s, *_: (s, 0, 0)),
                whole((1, 1)),
            ],
            scratch_shapes=[
                pltpu.VMEM((kern, GRID_X, 2 * GRID_Y), F32),
                pltpu.VMEM((2, freq_y, LANES), F32),
                pltpu.VMEM((2, freq_y, LANES), F32),
                pltpu.VMEM((GRID_X, GRID_Y), F32),
            ],
        ),
        out_shape=[
            jax.ShapeDtypeStruct((MOST, 72, LANES), F32),
            jax.ShapeDtypeStruct((1, 1), F32),
        ],
        compiler_params=pltpu.CompilerParams(vmem_limit_bytes=VMEM_BYTES),
        name="owner",
    )(ids, live, kern_weight, coeffs, targets, kernels[0], py, px, cs, wy)

    gathered = pl.pallas_call(
        functools.partial(collect_kernel, count),
        in_specs=[vmem],
        out_specs=vmem,
        out_shape=jax.ShapeDtypeStruct((count, MOST, 72, LANES), F32),
        scratch_shapes=[dma((count,))] * 2,
        compiler_params=pltpu.CompilerParams(
            collective_id=1, has_side_effects=True, vmem_limit_bytes=VMEM_BYTES
        ),
        name="collect",
    )(slopes)
    owners = owner_list[:, 0]
    same = owners[:, None] == owners[None, :]
    rank = jnp.sum(same & (places[None, :] < places[:, None]), axis=1).astype(jnp.int32)

    def slope_of(tile):
        inside = jnp.clip(tile, 0, count - 1)
        flat = gathered.reshape(count * MOST, 72, LANES)
        place = owners[inside] * MOST + rank[inside]
        found = lax.dynamic_index_in_dim(flat, place, 0, keepdims=False)
        return jnp.where(inside == tile, found, 0.0)

    my_slopes = jnp.stack([slope_of(me), slope_of(me + 1), slope_of(me - 1)])
    out = pl.pallas_call(
        update_kernel,
        grid=(steps,),
        in_specs=[
            pl.BlockSpec((1, chunk, tile_px), lambda i: (0, i, 0)),
            whole((3, 72, LANES)),
            pl.BlockSpec((chunk, 3 * ROWS), lambda i: (i, 0)),
            whole(col_tab.shape),
        ],
        out_specs=pl.BlockSpec((1, chunk, tile_px), lambda i: (0, i, 0)),
        out_shape=jax.ShapeDtypeStruct(mask_tiles.shape, F32),
        scratch_shapes=[pltpu.VMEM((3 * ROWS, tile_px), BF16)],
        compiler_params=pltpu.CompilerParams(vmem_limit_bytes=VMEM_BYTES),
        name="update",
    )(mask_tiles, my_slopes, row_bwd, col_tab)
    return out, (errors / (GRID_Y * CORE_X)).reshape(1)


def solution(mesh):
    placed = (
        P(("stripe", "tile"), None, None),
        P(("stripe", "tile"), None),
        P("tile", None, None, None, None),
        P(),
        P("stripe", None),
    )
    return jax.shard_map(
        on_device,
        mesh=mesh,
        in_specs=placed,
        out_specs=(P(("stripe", "tile"), None, None), P(("stripe", "tile"))),
        check_vma=False,
    )
```

```python
import functools

import jax
import jax.numpy as jnp
import ml_dtypes
import numpy as np
from jax import lax
from jax.experimental import pallas as pl
from jax.experimental.pallas import tpu as pltpu
from jax.sharding import PartitionSpec as P

AMBIT = 256
DIFF_STEPS = 2
GRID_X = 192
GRID_Y = 128
CORE_X = 128
MOST = 2
ROWS = 80
LANES = 128
VMEM_BYTES = 60 << 20

RESIST_SLOPE = 3.0
RESIST_LEVEL = 1.2
DIFFUSE_RATE = 0.2
STEP_SIZE = 1.0

F32 = jnp.float32
BF16 = jnp.bfloat16
HIGHEST = lax.Precision.HIGHEST


def angle(length, positions, freqs):
    turns = np.mod(np.outer(positions, freqs), length).astype(np.float64) / length
    return 2.0 * np.pi * turns


def halves(table):
    high = table.astype(np.float32).astype(ml_dtypes.bfloat16)
    low = (table - high.astype(np.float64)).astype(np.float32).astype(ml_dtypes.bfloat16)
    return high, low


def real_basis(length, count):
    half = count // 2
    return np.concatenate(
        [
            np.cos(angle(length, np.arange(length), np.arange(half + 1))),
            np.sin(angle(length, np.arange(length), np.arange(1, half + 1))),
        ],
        axis=1,
    )


def pickers(count, padded_freqs, padded_basis):
    half = count // 2
    cos_pick = np.zeros((padded_freqs, padded_basis), np.float32)
    sin_pick = np.zeros((padded_freqs, padded_basis), np.float32)
    for place in range(count):
        freq = place - half
        cos_pick[place, abs(freq)] = 1.0
        if freq:
            sin_pick[place, half + abs(freq)] = np.sign(freq)
    return cos_pick, sin_pick


def split(x):
    high = x.astype(BF16)
    low = (x - high.astype(F32)).astype(BF16)
    return high, low


def nn(a, b):
    return lax.dot_general(a, b, (((1,), (0,)), ((), ())), preferred_element_type=F32)


def nt(a, b):
    return lax.dot_general(a, b, (((1,), (1,)), ((), ())), preferred_element_type=F32)


def tn(a, b):
    return lax.dot_general(a, b, (((0,), (0,)), ((), ())), preferred_element_type=F32)


def nn3(a, b_high, b_low):
    a_high, a_low = split(a)
    return nn(a_high, b_high) + (nn(a_high, b_low) + nn(a_low, b_high))


def exact(dot, a, b):
    return lax.dot_general(a, b, dot, precision=HIGHEST, preferred_element_type=F32)


NN = (((1,), (0,)), ((), ()))
TN = (((0,), (0,)), ((), ()))
NT = (((1,), (1,)), ((), ()))


def coeffs_kernel(mask_ref, row_ref, col_ref, out_ref, total):
    step = pl.program_id(0)

    @pl.when(step == 0)
    def _():
        total[...] = jnp.zeros_like(total)

    m_high, m_low = split(mask_ref[0])
    both = nn(row_ref[...], m_high)
    total[...] += both[:ROWS] + (both[ROWS:] + nn(row_ref[:ROWS, :], m_low))

    @pl.when(step == pl.num_programs(0) - 1)
    def _():
        r_high, r_low = split(total[...])
        res = nn(r_high, col_ref[0]) + (nn(r_high, col_ref[1]) + nn(r_low, col_ref[0]))
        for piece in range(3):
            out_ref[piece] = res[:72, piece * LANES : (piece + 1) * LANES]


def update_kernel(mask_ref, owners_ref, slope_ref, row_ref, col_ref, out_ref, q_ref):
    @pl.when(pl.program_id(0) == 0)
    def _():
        count = slope_ref.shape[0]
        me = lax.axis_index("tile")

        def slope_of(tile):
            inside = jnp.clip(tile, 0, count - 1)
            owner = owners_ref[inside]
            rank = lax.fori_loop(
                0, inside, lambda i, r: jnp.where(owners_ref[i] == owner, 1, r), jnp.int32(0)
            )
            return jnp.where(inside == tile, slope_ref[owner, rank], 0.0)

        d = jnp.concatenate([slope_of(me), slope_of(me + 1), slope_of(me - 1)], axis=1)
        d = jnp.concatenate([d, jnp.zeros((ROWS - 72, 3 * LANES), F32)], axis=0)
        d_high, d_low = split(d)
        q = nt(d_high, col_ref[0]) + (nt(d_high, col_ref[1]) + nt(d_low, col_ref[0]))
        q_high, q_low = split(q)
        q_ref[:ROWS] = q_high
        q_ref[ROWS : 2 * ROWS] = q_high
        q_ref[2 * ROWS :] = q_low

    out_ref[0] = mask_ref[0] - STEP_SIZE * nn(row_ref[...], q_ref[...])


def diffuse(x):
    v_len, u_len = x.shape
    up = jnp.concatenate([x[:1], x[:-1]], axis=0)
    down = jnp.concatenate([x[1:], x[-1:]], axis=0)
    left = jnp.concatenate([x[:, :1], x[:, :-1]], axis=1)
    right = jnp.concatenate([x[:, 1:], x[:, -1:]], axis=1)
    return x + DIFFUSE_RATE * (up + down + left + right - 4.0 * x)


def owner_kernel(
    owners_ref, weight_ref, coeffs_ref, targets_ref, kern_ref, py_ref, px_ref, cs_ref, wy_ref,
    slope_ref, err_ref, amps, errors,
):
    freq_y, freq_x = kern_ref.shape[2], kern_ref.shape[3]
    kern = kern_ref.shape[1]
    count = coeffs_ref.shape[0]
    me = lax.axis_index("tile")

    def look(place, found):
        first, last = found
        mine = owners_ref[place] == me
        return (
            jnp.where(mine & (first == count), place, first),
            jnp.where(mine, place, last),
        )

    first, last = lax.fori_loop(0, count, look, (jnp.int32(count), jnp.int32(-1)))
    errors[...] = jnp.zeros_like(errors)

    def kern_pair(k):
        pad = jnp.zeros((freq_y, LANES - freq_x), F32)
        return (
            jnp.concatenate([kern_ref[0, k], pad], axis=1),
            jnp.concatenate([kern_ref[1, k], pad], axis=1),
        )

    def work(slot, carry):
        tile = jnp.where(slot == 0, first, last)
        live = jnp.where(slot == 0, first < count, last > first)

        @pl.when(jnp.logical_not(live))
        def _():
            slope_ref[slot] = jnp.zeros(slope_ref.shape[1:], F32)

        @pl.when(live)
        def _():
            one_tile(slot, tile)

        return carry

    def one_tile(slot, tile):
        u = exact(NN, py_ref[...], coeffs_ref[tile])
        u_cos, u_sin = u[:freq_y], u[freq_y:]
        px_cos, px_sin = px_ref[0], px_ref[1]
        spec_re = exact(NT, u_cos, px_cos) - exact(NT, u_sin, px_sin)
        spec_im = -(exact(NT, u_sin, px_cos) + exact(NT, u_cos, px_sin))
        total = jnp.zeros((GRID_X, GRID_Y), F32)
        for pair in range(kern // 2):
            rows = []
            for j in range(2):
                h_re, h_im = kern_pair(2 * pair + j)
                f_re = h_re * spec_re - h_im * spec_im
                f_im = h_re * spec_im + h_im * spec_re
                rows.append(jnp.concatenate([f_re, -f_im], axis=1))
                rows.append(jnp.concatenate([f_im, f_re], axis=1))
            f_high, f_low = split(jnp.concatenate(rows, axis=0))
            both = nt(cs_ref[...], f_high)
            x = both[:GRID_X] + (both[GRID_X:] + nt(cs_ref[:GRID_X, :], f_low))
            x_high, x_low = split(x)
            for j in range(2):
                k = 2 * pair + j
                part = slice(j * LANES, (j + 1) * LANES)
                xh, xl = x_high[:, part], x_low[:, part]
                amp = nn(jnp.concatenate([xh, xl, xh], axis=1), wy_ref[...])
                amps[k] = amp
                re, im = amp[:, :LANES], amp[:, LANES:]
                total = total + weight_ref[k] * (re * re + im * im)
        blurred = total
        for _ in range(DIFF_STEPS):
            blurred = diffuse(blurred)
        resist = 1.0 / (1.0 + jnp.exp(-RESIST_SLOPE * (blurred - RESIST_LEVEL)))
        offset = (GRID_X - CORE_X) // 2
        inner = resist[offset : offset + CORE_X]
        misfit = inner - targets_ref[tile].T
        errors[...] += jnp.sum(misfit * misfit, keepdims=True)
        core = (2.0 * RESIST_SLOPE) * misfit * inner * (1.0 - inner)
        edge = jnp.zeros((offset, GRID_Y), F32)
        slope = jnp.concatenate([edge, core, edge], axis=0)
        for _ in range(DIFF_STEPS):
            slope = diffuse(slope)
        slope = 2.0 * slope
        w_high = wy_ref[:LANES]
        w_both = wy_ref[LANES:]
        ds_re = jnp.zeros((freq_y, LANES), F32)
        ds_im = jnp.zeros((freq_y, LANES), F32)
        c_high, c_low = cs_ref[:GRID_X, :], cs_ref[GRID_X:, :]
        for k in range(kern):
            gain = weight_ref[k] * slope
            amp = amps[k]
            d = jnp.concatenate([gain * amp[:, :LANES], gain * amp[:, LANES:]], axis=1)
            d_high, d_low = split(d)
            both = nt(w_both, d_high)
            dx = both[:LANES] + (both[LANES:] + nt(w_high, d_low))
            x_high, x_low = split(dx)
            both = nn(jnp.concatenate([x_high, x_low], axis=0), c_high)
            df = both[:LANES] + (both[LANES:] + nn(x_high, c_low))
            d_re, d_im = df[:freq_y], df[freq_y:]
            f_re = d_re[:, :LANES] + d_im[:, LANES:]
            f_im = d_im[:, :LANES] - d_re[:, LANES:]
            h_re, h_im = kern_pair(k)
            ds_re = ds_re + (h_re * f_re + h_im * f_im)
            ds_im = ds_im + (h_re * f_im - h_im * f_re)
        du_cos = exact(NN, ds_re, px_cos) - exact(NN, ds_im, px_sin)
        du_sin = -(exact(NN, ds_re, px_sin) + exact(NN, ds_im, px_cos))
        slope_ref[slot] = exact(TN, py_ref[...], jnp.concatenate([du_cos, du_sin], axis=0))

    lax.fori_loop(0, MOST, work, 0)
    err_ref[...] = errors[...] * (1.0 / (GRID_Y * CORE_X))


def factors(count):
    pair = 2 if count % 2 == 0 else 1
    rest = count // pair
    inner = max(d for d in range(1, rest + 1) if rest % d == 0 and d * d <= rest)
    return rest // inner, inner, pair


def wrapped(index, size):
    return lax.rem(index + size, size)


class Place:
    def __init__(self, count):
        self.count = count
        self.outer, self.inner, self.pair = factors(count)
        self.me = lax.axis_index("tile")
        self.c = lax.rem(self.me, self.pair)
        self.b = lax.rem(self.me // self.pair, self.inner)
        self.a = self.me // (self.pair * self.inner)

    def at(self, da, db, dc):
        a = wrapped(self.a + da, self.outer)
        b = wrapped(self.b + db, self.inner)
        c = wrapped(self.c + dc, self.pair)
        return (a * self.inner + b) * self.pair + c

    def partners(self):
        return (
            [self.at(d, 0, 0) for d in range(1, self.outer)]
            + [self.at(0, d, 0) for d in range(1, self.inner)]
            + [self.at(0, 0, d) for d in range(1, self.pair)]
        )


def meet(devices):
    barrier = pltpu.get_barrier_semaphore()
    for device in devices:
        pl.semaphore_signal(
            barrier, inc=1, device_id={"tile": device}, device_id_type=pl.DeviceIdType.MESH
        )
    pl.semaphore_wait(barrier, len(devices))


class Gather:
    def __init__(self, place, slots, send, recv):
        self.place, self.slots, self.send, self.recv = place, slots, send, recv
        self.started = []

    def copy(self, slot, device, index):
        return pltpu.make_async_remote_copy(
            src_ref=self.slots.at[slot],
            dst_ref=self.slots.at[slot],
            send_sem=self.send.at[index],
            recv_sem=self.recv.at[slot],
            device_id={"tile": device},
            device_id_type=pl.DeviceIdType.MESH,
        )

    def push(self, slot, device):
        copy = self.copy(slot, device, len(self.started))
        copy.start()
        self.started.append(copy)

    def arrive(self, slot):
        self.copy(slot, self.place.at(1, 0, 0), 0).wait_recv()

    def to_pair(self, slot):
        for d in range(1, self.place.pair):
            self.push(slot, self.place.at(0, 0, d))

    def to_inner(self, slot):
        for d in range(1, self.place.inner):
            self.push(slot, self.place.at(0, d, 0))

    def own(self):
        p = self.place
        for d in range(1, p.outer):
            self.push(p.me, p.at(d, 0, 0))
        self.to_inner(p.me)
        self.to_pair(p.me)

    def outer_arrivals(self):
        for d in range(1, self.place.outer):
            slot = self.place.at(-d, 0, 0)
            self.arrive(slot)
            self.to_inner(slot)
            self.to_pair(slot)

    def inner_arrivals(self):
        for d in range(self.place.outer):
            for e in range(1, self.place.inner):
                slot = self.place.at(-d, -e, 0)
                self.arrive(slot)
                self.to_pair(slot)

    def finish(self):
        p = self.place
        for d in range(p.outer):
            for e in range(p.inner):
                for f in range(1, p.pair):
                    self.arrive(p.at(-d, -e, -f))
        for copy in self.started:
            copy.wait_send()


def spread_kernel(
    count, piece_ref, target_ref, coeff_ref, all_target_ref, near, near_send, near_recv,
    send_c, recv_c, send_t, recv_t,
):
    place = Place(count)
    me = place.me
    right, left = wrapped(me + 1, count), wrapped(me - 1, count)
    coeff = Gather(place, coeff_ref, send_c, recv_c)
    target = Gather(place, all_target_ref, send_t, recv_t)
    all_target_ref[me] = target_ref[...]
    meet([right, left] + place.partners())
    sides = []
    for side, device in ((0, right), (1, left)):
        copy = pltpu.make_async_remote_copy(
            src_ref=piece_ref.at[1 + side],
            dst_ref=near.at[side],
            send_sem=near_send.at[side],
            recv_sem=near_recv.at[side],
            device_id={"tile": device},
            device_id_type=pl.DeviceIdType.MESH,
        )
        copy.start()
        sides.append(copy)
    target.own()
    for copy in sides:
        copy.wait()
    own = piece_ref[0]
    own = own + jnp.where(me > 0, near[0], 0.0)
    own = own + jnp.where(me < count - 1, near[1], 0.0)
    coeff_ref[me] = own
    coeff.own()
    target.outer_arrivals()
    coeff.outer_arrivals()
    target.inner_arrivals()
    coeff.inner_arrivals()
    target.finish()
    coeff.finish()


def collect_kernel(count, slope_ref, all_ref, send, recv):
    place = Place(count)
    gather = Gather(place, all_ref, send, recv)
    all_ref[place.me] = slope_ref[...]
    meet(place.partners())
    gather.own()
    gather.outer_arrivals()
    gather.inner_arrivals()
    gather.finish()


def tables(tile_px, freq_y, freq_x):
    win = tile_px + 2 * AMBIT
    row = np.zeros((tile_px, ROWS))
    row[:, : freq_y + 1] = real_basis(tile_px, freq_y)
    col = np.zeros((win, LANES))
    col[:, : freq_x + 1] = real_basis(win, freq_x)
    pieces = np.zeros((tile_px, 3 * LANES))
    pieces[:, :LANES] = col[AMBIT : AMBIT + tile_px]
    pieces[tile_px - AMBIT :, LANES : 2 * LANES] = col[:AMBIT]
    pieces[:AMBIT, 2 * LANES :] = col[AMBIT + tile_px :]
    r_high, r_low = halves(row)
    row_fwd = np.concatenate([r_high.T, r_low.T], axis=0)
    row_bwd = np.concatenate([r_high, r_low, r_high], axis=1)
    col_tab = np.stack(halves(pieces))
    py = np.concatenate(pickers(freq_y, freq_y, 72), axis=0)
    px = np.stack(pickers(freq_x, LANES, LANES))
    ax = angle(GRID_X, np.arange(GRID_X), np.arange(freq_x) - freq_x // 2)
    cs = np.zeros((GRID_X, 2 * LANES))
    cs[:, :freq_x] = np.cos(ax)
    cs[:, LANES : LANES + freq_x] = np.sin(ax)
    cs = np.concatenate(halves(cs), axis=0)
    ay = angle(GRID_Y, np.arange(freq_y) - freq_y // 2, np.arange(GRID_Y))
    wy = np.block([[np.cos(ay), np.sin(ay)], [-np.sin(ay), np.cos(ay)]]) / (64.0 * GRID_Y * GRID_X)
    w_high, w_low = halves(wy)
    wy = np.concatenate([w_high, w_high, w_low], axis=0)
    return row_fwd, row_bwd, col_tab, py, px, cs, wy


def whole(shape, memory_space=None):
    return pl.BlockSpec(shape, lambda *_: (0,) * len(shape))


def on_device(mask_tiles, target_grid, kernels, kern_weight, owner_list):
    tile_px = mask_tiles.shape[1]
    kern, freq_y, freq_x = kernels.shape[2:]
    count = lax.axis_size("tile")
    row_fwd, row_bwd, col_tab, py, px, cs, wy = tables(tile_px, freq_y, freq_x)

    chunk = 256
    steps = tile_px // chunk
    pieces = pl.pallas_call(
        coeffs_kernel,
        grid=(steps,),
        in_specs=[
            pl.BlockSpec((1, chunk, tile_px), lambda i: (0, i, 0)),
            pl.BlockSpec((2 * ROWS, chunk), lambda i: (0, i)),
            whole(col_tab.shape),
        ],
        out_specs=whole((3, 72, LANES)),
        out_shape=jax.ShapeDtypeStruct((3, 72, LANES), F32),
        scratch_shapes=[pltpu.VMEM((ROWS, tile_px), F32)],
        compiler_params=pltpu.CompilerParams(vmem_limit_bytes=VMEM_BYTES),
        name="coeffs",
    )(mask_tiles, row_fwd, col_tab)

    vmem = pl.BlockSpec(memory_space=pltpu.VMEM)
    dma = pltpu.SemaphoreType.DMA
    coeffs, targets = pl.pallas_call(
        functools.partial(spread_kernel, count),
        in_specs=[vmem, vmem],
        out_specs=[vmem, vmem],
        out_shape=[
            jax.ShapeDtypeStruct((count, 72, LANES), F32),
            jax.ShapeDtypeStruct((count, GRID_Y, CORE_X), F32),
        ],
        scratch_shapes=[pltpu.VMEM((2, 72, LANES), F32), dma((2,)), dma((2,))]
        + [dma((count,))] * 4,
        compiler_params=pltpu.CompilerParams(
            collective_id=0, has_side_effects=True, vmem_limit_bytes=VMEM_BYTES
        ),
        name="spread",
    )(pieces, target_grid.reshape(GRID_Y, CORE_X))

    smem = pl.BlockSpec(memory_space=pltpu.SMEM)
    owners = owner_list[:, 0]
    slopes, errors = pl.pallas_call(
        owner_kernel,
        in_specs=[smem, smem] + [vmem] * 7,
        out_specs=[vmem, vmem],
        out_shape=[
            jax.ShapeDtypeStruct((MOST, 72, LANES), F32),
            jax.ShapeDtypeStruct((1, 1), F32),
        ],
        scratch_shapes=[
            pltpu.VMEM((kern, GRID_X, 2 * GRID_Y), F32),
            pltpu.VMEM((1, 1), F32),
        ],
        compiler_params=pltpu.CompilerParams(vmem_limit_bytes=VMEM_BYTES),
        name="owner",
    )(owners, kern_weight, coeffs, targets, kernels[0], py, px, cs, wy)

    gathered = pl.pallas_call(
        functools.partial(collect_kernel, count),
        in_specs=[vmem],
        out_specs=vmem,
        out_shape=jax.ShapeDtypeStruct((count, MOST, 72, LANES), F32),
        scratch_shapes=[dma((count,))] * 2,
        compiler_params=pltpu.CompilerParams(
            collective_id=1, has_side_effects=True, vmem_limit_bytes=VMEM_BYTES
        ),
        name="collect",
    )(slopes)
    out = pl.pallas_call(
        update_kernel,
        grid=(steps,),
        in_specs=[
            pl.BlockSpec((1, chunk, tile_px), lambda i: (0, i, 0)),
            smem,
            whole((count, MOST, 72, LANES)),
            pl.BlockSpec((chunk, 3 * ROWS), lambda i: (i, 0)),
            whole(col_tab.shape),
        ],
        out_specs=pl.BlockSpec((1, chunk, tile_px), lambda i: (0, i, 0)),
        out_shape=jax.ShapeDtypeStruct(mask_tiles.shape, F32),
        scratch_shapes=[pltpu.VMEM((3 * ROWS, tile_px), BF16)],
        compiler_params=pltpu.CompilerParams(vmem_limit_bytes=VMEM_BYTES),
        name="update",
    )(mask_tiles, owners, gathered, row_bwd, col_tab)
    return out, errors.reshape(1)


def solution(mesh):
    placed = (
        P(("stripe", "tile"), None, None),
        P(("stripe", "tile"), None),
        P("tile", None, None, None, None),
        P(),
        P("stripe", None),
    )
    return jax.shard_map(
        on_device,
        mesh=mesh,
        in_specs=placed,
        out_specs=(P(("stripe", "tile"), None, None), P(("stripe", "tile"))),
        check_vma=False,
    )
```

```python
import functools

import jax
import jax.numpy as jnp
import ml_dtypes
import numpy as np
from jax import lax
from jax.experimental import pallas as pl
from jax.experimental.pallas import tpu as pltpu
from jax.sharding import PartitionSpec as P

AMBIT = 256
DIFF_STEPS = 2
GRID_X = 192
GRID_Y = 128
CORE_X = 128
MOST = 2
PARTS = 2
GROUP = 4
ROWS = 80
LANES = 128
VMEM_BYTES = 60 << 20

RESIST_SLOPE = 3.0
RESIST_LEVEL = 1.2
DIFFUSE_RATE = 0.2
STEP_SIZE = 1.0

F32 = jnp.float32
BF16 = jnp.bfloat16
HIGHEST = lax.Precision.HIGHEST


def angle(length, positions, freqs):
    turns = np.mod(np.outer(positions, freqs), length).astype(np.float64) / length
    return 2.0 * np.pi * turns


def halves(table):
    high = table.astype(np.float32).astype(ml_dtypes.bfloat16)
    low = (table - high.astype(np.float64)).astype(np.float32).astype(ml_dtypes.bfloat16)
    return high, low


def real_basis(length, count):
    half = count // 2
    return np.concatenate(
        [
            np.cos(angle(length, np.arange(length), np.arange(half + 1))),
            np.sin(angle(length, np.arange(length), np.arange(1, half + 1))),
        ],
        axis=1,
    )


def pickers(count, padded_freqs, padded_basis):
    half = count // 2
    cos_pick = np.zeros((padded_freqs, padded_basis), np.float32)
    sin_pick = np.zeros((padded_freqs, padded_basis), np.float32)
    for place in range(count):
        freq = place - half
        cos_pick[place, abs(freq)] = 1.0
        if freq:
            sin_pick[place, half + abs(freq)] = np.sign(freq)
    return cos_pick, sin_pick


def split(x):
    high = x.astype(BF16)
    low = (x - high.astype(F32)).astype(BF16)
    return high, low


def nn(a, b):
    return lax.dot_general(a, b, (((1,), (0,)), ((), ())), preferred_element_type=F32)


def nt(a, b):
    return lax.dot_general(a, b, (((1,), (1,)), ((), ())), preferred_element_type=F32)


def tn(a, b):
    return lax.dot_general(a, b, (((0,), (0,)), ((), ())), preferred_element_type=F32)


def nn3(a, b_high, b_low):
    a_high, a_low = split(a)
    return nn(a_high, b_high) + (nn(a_high, b_low) + nn(a_low, b_high))


def exact(dot, a, b):
    return lax.dot_general(a, b, dot, precision=HIGHEST, preferred_element_type=F32)


NN = (((1,), (0,)), ((), ()))
TN = (((0,), (0,)), ((), ()))
NT = (((1,), (1,)), ((), ()))


def coeffs_kernel(mask_ref, row_ref, col_ref, out_ref, total):
    step = pl.program_id(0)

    @pl.when(step == 0)
    def _():
        total[...] = jnp.zeros_like(total)

    m_high, m_low = split(mask_ref[0])
    both = nn(row_ref[...], m_high)
    total[...] += both[:ROWS] + (both[ROWS:] + nn(row_ref[:ROWS, :], m_low))

    @pl.when(step == pl.num_programs(0) - 1)
    def _():
        r_high, r_low = split(total[...])
        res = nn(r_high, col_ref[0]) + (nn(r_high, col_ref[1]) + nn(r_low, col_ref[0]))
        for piece in range(3):
            out_ref[piece] = res[:72, piece * LANES : (piece + 1) * LANES]


def update_kernel(mask_ref, owners_ref, slope_ref, row_ref, col_ref, out_ref, q_ref):
    @pl.when(pl.program_id(0) == 0)
    def _():
        count = slope_ref.shape[1]
        me = lax.axis_index("tile")

        def slope_of(tile):
            inside = jnp.clip(tile, 0, count - 1)
            owner = owners_ref[inside]
            rank = lax.fori_loop(
                0, inside, lambda i, r: jnp.where(owners_ref[i] == owner, 1, r), jnp.int32(0)
            )
            return jnp.where(inside == tile, slope_ref[rank, owner], 0.0)

        d = jnp.concatenate([slope_of(me), slope_of(me + 1), slope_of(me - 1)], axis=1)
        d = jnp.concatenate([d, jnp.zeros((ROWS - 72, 3 * LANES), F32)], axis=0)
        d_high, d_low = split(d)
        q = nt(d_high, col_ref[0]) + (nt(d_high, col_ref[1]) + nt(d_low, col_ref[0]))
        q_high, q_low = split(q)
        q_ref[:ROWS] = q_high
        q_ref[ROWS : 2 * ROWS] = q_high
        q_ref[2 * ROWS :] = q_low

    out_ref[0] = mask_ref[0] - STEP_SIZE * nn(row_ref[...], q_ref[...])


def diffuse(x):
    v_len, u_len = x.shape
    up = jnp.concatenate([x[:1], x[:-1]], axis=0)
    down = jnp.concatenate([x[1:], x[-1:]], axis=0)
    left = jnp.concatenate([x[:, :1], x[:, :-1]], axis=1)
    right = jnp.concatenate([x[:, 1:], x[:, -1:]], axis=1)
    return x + DIFFUSE_RATE * (up + down + left + right - 4.0 * x)


def owner_kernel(
    owners_ref, weight_ref, coeffs_ref, targets_ref, kern_ref, py_ref, px_ref, cs_ref, wy_ref,
    slope_ref, err_ref, amps, errors,
):
    freq_y, freq_x = kern_ref.shape[2], kern_ref.shape[3]
    kern = kern_ref.shape[1]
    count = coeffs_ref.shape[0]
    me = lax.axis_index("tile")

    def look(place, found):
        first, last = found
        mine = owners_ref[place] == me
        return (
            jnp.where(mine & (first == count), place, first),
            jnp.where(mine, place, last),
        )

    first, last = lax.fori_loop(0, count, look, (jnp.int32(count), jnp.int32(-1)))
    errors[...] = jnp.zeros_like(errors)

    def kern_pair(k):
        pad = jnp.zeros((freq_y, LANES - freq_x), F32)
        return (
            jnp.concatenate([kern_ref[0, k], pad], axis=1),
            jnp.concatenate([kern_ref[1, k], pad], axis=1),
        )

    def work(slot, carry):
        tile = jnp.where(slot == 0, first, last)
        live = jnp.where(slot == 0, first < count, last > first)

        @pl.when(jnp.logical_not(live))
        def _():
            slope_ref[slot] = jnp.zeros(slope_ref.shape[1:], F32)

        @pl.when(live)
        def _():
            one_tile(slot, tile)

        return carry

    def one_tile(slot, tile):
        u = exact(NN, py_ref[...], coeffs_ref[tile])
        u_cos, u_sin = u[:freq_y], u[freq_y:]
        px_cos, px_sin = px_ref[0], px_ref[1]
        spec_re = exact(NT, u_cos, px_cos) - exact(NT, u_sin, px_sin)
        spec_im = -(exact(NT, u_sin, px_cos) + exact(NT, u_cos, px_sin))
        total = jnp.zeros((GRID_X, GRID_Y), F32)
        for pair in range(kern // 2):
            rows = []
            for j in range(2):
                h_re, h_im = kern_pair(2 * pair + j)
                f_re = h_re * spec_re - h_im * spec_im
                f_im = h_re * spec_im + h_im * spec_re
                rows.append(jnp.concatenate([f_re, -f_im], axis=1))
                rows.append(jnp.concatenate([f_im, f_re], axis=1))
            f_high, f_low = split(jnp.concatenate(rows, axis=0))
            both = nt(cs_ref[...], f_high)
            x = both[:GRID_X] + (both[GRID_X:] + nt(cs_ref[:GRID_X, :], f_low))
            x_high, x_low = split(x)
            for j in range(2):
                k = 2 * pair + j
                part = slice(j * LANES, (j + 1) * LANES)
                xh, xl = x_high[:, part], x_low[:, part]
                amp = nn(jnp.concatenate([xh, xl, xh], axis=1), wy_ref[...])
                amps[k] = amp
                re, im = amp[:, :LANES], amp[:, LANES:]
                total = total + weight_ref[k] * (re * re + im * im)
        blurred = total
        for _ in range(DIFF_STEPS):
            blurred = diffuse(blurred)
        resist = 1.0 / (1.0 + jnp.exp(-RESIST_SLOPE * (blurred - RESIST_LEVEL)))
        offset = (GRID_X - CORE_X) // 2
        inner = resist[offset : offset + CORE_X]
        target = jnp.concatenate([targets_ref[part, tile] for part in range(PARTS)], axis=0)
        misfit = inner - target.T
        errors[...] += jnp.sum(misfit * misfit, keepdims=True)
        core = (2.0 * RESIST_SLOPE) * misfit * inner * (1.0 - inner)
        edge = jnp.zeros((offset, GRID_Y), F32)
        slope = jnp.concatenate([edge, core, edge], axis=0)
        for _ in range(DIFF_STEPS):
            slope = diffuse(slope)
        slope = 2.0 * slope
        ds_re = jnp.zeros((freq_y, LANES), F32)
        ds_im = jnp.zeros((freq_y, LANES), F32)
        c_high, c_low = cs_ref[:GRID_X, :], cs_ref[GRID_X:, :]
        for base in range(0, kern, GROUP):
            grads = []
            for k in range(base, base + GROUP):
                gain = weight_ref[k] * slope
                amp = amps[k]
                grads.append(jnp.concatenate([gain * amp[:, :LANES], gain * amp[:, LANES:]], axis=1))
            d_high, d_low = split(jnp.concatenate(grads, axis=0))
            both = nt(d_high, wy_ref[LANES:])
            dx = both[:, :LANES] + (both[:, LANES:] + nt(d_low, wy_ref[:LANES]))
            flipped = [dx[j * GRID_X : (j + 1) * GRID_X].T for j in range(GROUP)]
            x_high, x_low = split(jnp.concatenate(flipped, axis=0))
            df_all = nn(x_high, c_high) + (nn(x_high, c_low) + nn(x_low, c_high))
            for j in range(GROUP):
                df = df_all[j * LANES : (j + 1) * LANES]
                d_re, d_im = df[:freq_y], df[freq_y:]
                f_re = d_re[:, :LANES] + d_im[:, LANES:]
                f_im = d_im[:, :LANES] - d_re[:, LANES:]
                h_re, h_im = kern_pair(base + j)
                ds_re = ds_re + (h_re * f_re + h_im * f_im)
                ds_im = ds_im + (h_re * f_im - h_im * f_re)
        du_cos = exact(NN, ds_re, px_cos) - exact(NN, ds_im, px_sin)
        du_sin = -(exact(NN, ds_re, px_sin) + exact(NN, ds_im, px_cos))
        slope_ref[slot] = exact(TN, py_ref[...], jnp.concatenate([du_cos, du_sin], axis=0))

    lax.fori_loop(0, MOST, work, 0)
    err_ref[...] = errors[...] * (1.0 / (GRID_Y * CORE_X))


def factors(count):
    pair = 2 if count % 2 == 0 else 1
    rest = count // pair
    inner = max(d for d in range(1, rest + 1) if rest % d == 0 and d * d <= rest)
    return rest // inner, inner, pair


def wrapped(index, size):
    return lax.rem(index + size, size)


class Place:
    def __init__(self, count):
        self.count = count
        self.outer, self.inner, self.pair = factors(count)
        self.me = lax.axis_index("tile")
        self.c = lax.rem(self.me, self.pair)
        self.b = lax.rem(self.me // self.pair, self.inner)
        self.a = self.me // (self.pair * self.inner)

    def at(self, da, db, dc):
        a = wrapped(self.a + da, self.outer)
        b = wrapped(self.b + db, self.inner)
        c = wrapped(self.c + dc, self.pair)
        return (a * self.inner + b) * self.pair + c

    def partners(self):
        return (
            [self.at(d, 0, 0) for d in range(1, self.outer)]
            + [self.at(0, d, 0) for d in range(1, self.inner)]
            + [self.at(0, 0, d) for d in range(1, self.pair)]
        )


def meet(devices):
    barrier = pltpu.get_barrier_semaphore()
    for device in devices:
        pl.semaphore_signal(
            barrier, inc=1, device_id={"tile": device}, device_id_type=pl.DeviceIdType.MESH
        )
    pl.semaphore_wait(barrier, len(devices))


class Gather:
    def __init__(self, place, slots, send, recv):
        self.place, self.slots, self.send, self.recv = place, slots, send, recv
        self.started = []

    def copy(self, slot, device, index):
        return pltpu.make_async_remote_copy(
            src_ref=self.slots.at[slot],
            dst_ref=self.slots.at[slot],
            send_sem=self.send.at[index],
            recv_sem=self.recv.at[slot],
            device_id={"tile": device},
            device_id_type=pl.DeviceIdType.MESH,
        )

    def push(self, slot, device):
        copy = self.copy(slot, device, len(self.started))
        copy.start()
        self.started.append(copy)

    def arrive(self, slot):
        self.copy(slot, self.place.at(1, 0, 0), 0).wait_recv()

    def to_pair(self, slot):
        for d in range(1, self.place.pair):
            self.push(slot, self.place.at(0, 0, d))

    def to_inner(self, slot):
        for d in range(1, self.place.inner):
            self.push(slot, self.place.at(0, d, 0))

    def own(self):
        p = self.place
        for d in range(1, p.outer):
            self.push(p.me, p.at(d, 0, 0))
        self.to_inner(p.me)
        self.to_pair(p.me)

    def outer_arrivals(self):
        for d in range(1, self.place.outer):
            slot = self.place.at(-d, 0, 0)
            self.arrive(slot)
            self.to_inner(slot)
            self.to_pair(slot)

    def inner_arrivals(self):
        for d in range(self.place.outer):
            for e in range(1, self.place.inner):
                slot = self.place.at(-d, -e, 0)
                self.arrive(slot)
                self.to_pair(slot)

    def finish(self):
        p = self.place
        for d in range(p.outer):
            for e in range(p.inner):
                for f in range(1, p.pair):
                    self.arrive(p.at(-d, -e, -f))
        for copy in self.started:
            copy.wait_send()


def spread_kernel(
    count, piece_ref, target_ref, coeff_ref, all_target_ref, near, near_send, near_recv,
    send_c, recv_c, *sems,
):
    place = Place(count)
    me = place.me
    right, left = wrapped(me + 1, count), wrapped(me - 1, count)
    coeff = Gather(place, coeff_ref, send_c, recv_c)
    targets = []
    for part in range(PARTS):
        targets.append(Gather(place, all_target_ref.at[part], sems[2 * part], sems[2 * part + 1]))
        all_target_ref[part, me] = target_ref[part]
    meet([right, left] + place.partners())
    sides = []
    for side, device in ((0, right), (1, left)):
        copy = pltpu.make_async_remote_copy(
            src_ref=piece_ref.at[1 + side],
            dst_ref=near.at[side],
            send_sem=near_send.at[side],
            recv_sem=near_recv.at[side],
            device_id={"tile": device},
            device_id_type=pl.DeviceIdType.MESH,
        )
        copy.start()
        sides.append(copy)
    for target in targets:
        target.own()
    for copy in sides:
        copy.wait()
    own = piece_ref[0]
    own = own + jnp.where(me > 0, near[0], 0.0)
    own = own + jnp.where(me < count - 1, near[1], 0.0)
    coeff_ref[me] = own
    coeff.own()
    forward(targets + [coeff])


def collect_kernel(count, slope_ref, all_ref, *sems):
    place = Place(count)
    gathers = [
        Gather(place, all_ref.at[slot], sems[2 * slot], sems[2 * slot + 1]) for slot in range(MOST)
    ]
    for slot in range(MOST):
        all_ref[slot, place.me] = slope_ref[slot]
    meet(place.partners())
    together(gathers)


def together(gathers):
    for gather in gathers:
        gather.own()
    forward(gathers)


def forward(gathers):
    for gather in gathers:
        gather.outer_arrivals()
    for gather in gathers:
        gather.inner_arrivals()
    for gather in gathers:
        gather.finish()


def tables(tile_px, freq_y, freq_x):
    win = tile_px + 2 * AMBIT
    row = np.zeros((tile_px, ROWS))
    row[:, : freq_y + 1] = real_basis(tile_px, freq_y)
    col = np.zeros((win, LANES))
    col[:, : freq_x + 1] = real_basis(win, freq_x)
    pieces = np.zeros((tile_px, 3 * LANES))
    pieces[:, :LANES] = col[AMBIT : AMBIT + tile_px]
    pieces[tile_px - AMBIT :, LANES : 2 * LANES] = col[:AMBIT]
    pieces[:AMBIT, 2 * LANES :] = col[AMBIT + tile_px :]
    r_high, r_low = halves(row)
    row_fwd = np.concatenate([r_high.T, r_low.T], axis=0)
    row_bwd = np.concatenate([r_high, r_low, r_high], axis=1)
    col_tab = np.stack(halves(pieces))
    py = np.concatenate(pickers(freq_y, freq_y, 72), axis=0)
    px = np.stack(pickers(freq_x, LANES, LANES))
    ax = angle(GRID_X, np.arange(GRID_X), np.arange(freq_x) - freq_x // 2)
    cs = np.zeros((GRID_X, 2 * LANES))
    cs[:, :freq_x] = np.cos(ax)
    cs[:, LANES : LANES + freq_x] = np.sin(ax)
    cs = np.concatenate(halves(cs), axis=0)
    ay = angle(GRID_Y, np.arange(freq_y) - freq_y // 2, np.arange(GRID_Y))
    wy = np.block([[np.cos(ay), np.sin(ay)], [-np.sin(ay), np.cos(ay)]]) / (64.0 * GRID_Y * GRID_X)
    w_high, w_low = halves(wy)
    wy = np.concatenate([w_high, w_high, w_low], axis=0)
    return row_fwd, row_bwd, col_tab, py, px, cs, wy


def whole(shape, memory_space=None):
    return pl.BlockSpec(shape, lambda *_: (0,) * len(shape))


def on_device(mask_tiles, target_grid, kernels, kern_weight, owner_list):
    tile_px = mask_tiles.shape[1]
    kern, freq_y, freq_x = kernels.shape[2:]
    count = lax.axis_size("tile")
    row_fwd, row_bwd, col_tab, py, px, cs, wy = tables(tile_px, freq_y, freq_x)

    chunk = 256
    steps = tile_px // chunk
    pieces = pl.pallas_call(
        coeffs_kernel,
        grid=(steps,),
        in_specs=[
            pl.BlockSpec((1, chunk, tile_px), lambda i: (0, i, 0)),
            pl.BlockSpec((2 * ROWS, chunk), lambda i: (0, i)),
            whole(col_tab.shape),
        ],
        out_specs=whole((3, 72, LANES)),
        out_shape=jax.ShapeDtypeStruct((3, 72, LANES), F32),
        scratch_shapes=[pltpu.VMEM((ROWS, tile_px), F32)],
        compiler_params=pltpu.CompilerParams(vmem_limit_bytes=VMEM_BYTES),
        name="coeffs",
    )(mask_tiles, row_fwd, col_tab)

    vmem = pl.BlockSpec(memory_space=pltpu.VMEM)
    dma = pltpu.SemaphoreType.DMA
    coeffs, targets = pl.pallas_call(
        functools.partial(spread_kernel, count),
        in_specs=[vmem, vmem],
        out_specs=[vmem, vmem],
        out_shape=[
            jax.ShapeDtypeStruct((count, 72, LANES), F32),
            jax.ShapeDtypeStruct((PARTS, count, GRID_Y // PARTS, CORE_X), F32),
        ],
        scratch_shapes=[pltpu.VMEM((2, 72, LANES), F32), dma((2,)), dma((2,))]
        + [dma((count,))] * (2 + 2 * PARTS),
        compiler_params=pltpu.CompilerParams(
            collective_id=0, has_side_effects=True, vmem_limit_bytes=VMEM_BYTES
        ),
        name="spread",
    )(pieces, target_grid.reshape(PARTS, GRID_Y // PARTS, CORE_X))

    smem = pl.BlockSpec(memory_space=pltpu.SMEM)
    owners = owner_list[:, 0]
    slopes, errors = pl.pallas_call(
        owner_kernel,
        in_specs=[smem, smem] + [vmem] * 7,
        out_specs=[vmem, vmem],
        out_shape=[
            jax.ShapeDtypeStruct((MOST, 72, LANES), F32),
            jax.ShapeDtypeStruct((1, 1), F32),
        ],
        scratch_shapes=[
            pltpu.VMEM((kern, GRID_X, 2 * GRID_Y), F32),
            pltpu.VMEM((1, 1), F32),
        ],
        compiler_params=pltpu.CompilerParams(vmem_limit_bytes=VMEM_BYTES),
        name="owner",
    )(owners, kern_weight, coeffs, targets, kernels[0], py, px, cs, wy)

    gathered = pl.pallas_call(
        functools.partial(collect_kernel, count),
        in_specs=[vmem],
        out_specs=vmem,
        out_shape=jax.ShapeDtypeStruct((MOST, count, 72, LANES), F32),
        scratch_shapes=[dma((count,))] * (2 * MOST),
        compiler_params=pltpu.CompilerParams(
            collective_id=1, has_side_effects=True, vmem_limit_bytes=VMEM_BYTES
        ),
        name="collect",
    )(slopes)
    out = pl.pallas_call(
        update_kernel,
        grid=(steps,),
        in_specs=[
            pl.BlockSpec((1, chunk, tile_px), lambda i: (0, i, 0)),
            smem,
            whole((MOST, count, 72, LANES)),
            pl.BlockSpec((chunk, 3 * ROWS), lambda i: (i, 0)),
            whole(col_tab.shape),
        ],
        out_specs=pl.BlockSpec((1, chunk, tile_px), lambda i: (0, i, 0)),
        out_shape=jax.ShapeDtypeStruct(mask_tiles.shape, F32),
        scratch_shapes=[pltpu.VMEM((3 * ROWS, tile_px), BF16)],
        compiler_params=pltpu.CompilerParams(vmem_limit_bytes=VMEM_BYTES),
        name="update",
    )(mask_tiles, owners, gathered, row_bwd, col_tab)
    return out, errors.reshape(1)


def solution(mesh):
    placed = (
        P(("stripe", "tile"), None, None),
        P(("stripe", "tile"), None),
        P("tile", None, None, None, None),
        P(),
        P("stripe", None),
    )
    return jax.shard_map(
        on_device,
        mesh=mesh,
        in_specs=placed,
        out_specs=(P(("stripe", "tile"), None, None), P(("stripe", "tile"))),
        check_vma=False,
    )
```

```python
import functools

import jax
import jax.numpy as jnp
import ml_dtypes
import numpy as np
from jax import lax
from jax.experimental import pallas as pl
from jax.experimental.pallas import tpu as pltpu
from jax.sharding import PartitionSpec as P

AMBIT = 256
DIFF_STEPS = 2
GRID_X = 192
GRID_Y = 128
CORE_X = 128
MOST = 2
PARTS = 2
GROUP = 4
ROWS = 80
LANES = 128
VMEM_BYTES = 60 << 20

RESIST_SLOPE = 3.0
RESIST_LEVEL = 1.2
DIFFUSE_RATE = 0.2
STEP_SIZE = 1.0

F32 = jnp.float32
BF16 = jnp.bfloat16
HIGHEST = lax.Precision.HIGHEST


def angle(length, positions, freqs):
    turns = np.mod(np.outer(positions, freqs), length).astype(np.float64) / length
    return 2.0 * np.pi * turns


def halves(table):
    high = table.astype(np.float32).astype(ml_dtypes.bfloat16)
    low = (table - high.astype(np.float64)).astype(np.float32).astype(ml_dtypes.bfloat16)
    return high, low


def real_basis(length, count):
    half = count // 2
    return np.concatenate(
        [
            np.cos(angle(length, np.arange(length), np.arange(half + 1))),
            np.sin(angle(length, np.arange(length), np.arange(1, half + 1))),
        ],
        axis=1,
    )


def pickers(count, padded_freqs, padded_basis):
    half = count // 2
    cos_pick = np.zeros((padded_freqs, padded_basis), np.float32)
    sin_pick = np.zeros((padded_freqs, padded_basis), np.float32)
    for place in range(count):
        freq = place - half
        cos_pick[place, abs(freq)] = 1.0
        if freq:
            sin_pick[place, half + abs(freq)] = np.sign(freq)
    return cos_pick, sin_pick


def split(x):
    high = x.astype(BF16)
    low = (x - high.astype(F32)).astype(BF16)
    return high, low


def nn(a, b):
    return lax.dot_general(a, b, (((1,), (0,)), ((), ())), preferred_element_type=F32)


def nt(a, b):
    return lax.dot_general(a, b, (((1,), (1,)), ((), ())), preferred_element_type=F32)


def tn(a, b):
    return lax.dot_general(a, b, (((0,), (0,)), ((), ())), preferred_element_type=F32)


def nn3(a, b_high, b_low):
    a_high, a_low = split(a)
    return nn(a_high, b_high) + (nn(a_high, b_low) + nn(a_low, b_high))


def exact(dot, a, b):
    return lax.dot_general(a, b, dot, precision=HIGHEST, preferred_element_type=F32)


NN = (((1,), (0,)), ((), ()))
TN = (((0,), (0,)), ((), ()))
NT = (((1,), (1,)), ((), ()))


def coeffs_kernel(mask_ref, row_ref, col_ref, out_ref, total):
    step = pl.program_id(0)

    @pl.when(step == 0)
    def _():
        total[...] = jnp.zeros_like(total)

    m_high, m_low = split(mask_ref[0])
    both = nn(row_ref[...], m_high)
    total[...] += both[:ROWS] + (both[ROWS:] + nn(row_ref[:ROWS, :], m_low))

    @pl.when(step == pl.num_programs(0) - 1)
    def _():
        r_high, r_low = split(total[...])
        res = nn(r_high, col_ref[0]) + (nn(r_high, col_ref[1]) + nn(r_low, col_ref[0]))
        for piece in range(3):
            out_ref[piece] = res[:72, piece * LANES : (piece + 1) * LANES]


def update_kernel(mask_ref, owners_ref, slope_ref, row_ref, col_ref, out_ref, q_ref):
    @pl.when(pl.program_id(0) == 0)
    def _():
        count = slope_ref.shape[1]
        me = lax.axis_index("tile")

        def slope_of(tile):
            inside = jnp.clip(tile, 0, count - 1)
            owner = owners_ref[inside]
            rank = lax.fori_loop(
                0, inside, lambda i, r: jnp.where(owners_ref[i] == owner, 1, r), jnp.int32(0)
            )
            return jnp.where(inside == tile, slope_ref[rank, owner], 0.0)

        d = jnp.concatenate([slope_of(me), slope_of(me + 1), slope_of(me - 1)], axis=1)
        d = jnp.concatenate([d, jnp.zeros((ROWS - 72, 3 * LANES), F32)], axis=0)
        d_high, d_low = split(d)
        q = nt(d_high, col_ref[0]) + (nt(d_high, col_ref[1]) + nt(d_low, col_ref[0]))
        q_high, q_low = split(q)
        q_ref[:ROWS] = q_high
        q_ref[ROWS : 2 * ROWS] = q_high
        q_ref[2 * ROWS :] = q_low

    out_ref[0] = mask_ref[0] - STEP_SIZE * nn(row_ref[...], q_ref[...])


def diffuse(x):
    v_len, u_len = x.shape
    up = jnp.concatenate([x[:1], x[:-1]], axis=0)
    down = jnp.concatenate([x[1:], x[-1:]], axis=0)
    left = jnp.concatenate([x[:, :1], x[:, :-1]], axis=1)
    right = jnp.concatenate([x[:, 1:], x[:, -1:]], axis=1)
    return x + DIFFUSE_RATE * (up + down + left + right - 4.0 * x)


def owner_kernel(
    owners_ref, weight_ref, coeffs_ref, targets_ref, kern_ref, py_ref, px_ref, cs_ref, wy_ref,
    slope_ref, err_ref, amps, errors,
):
    freq_y, freq_x = kern_ref.shape[2], kern_ref.shape[3]
    kern = kern_ref.shape[1]
    count = coeffs_ref.shape[0]
    me = lax.axis_index("tile")

    def look(place, found):
        first, last = found
        mine = owners_ref[place] == me
        return (
            jnp.where(mine & (first == count), place, first),
            jnp.where(mine, place, last),
        )

    first, last = lax.fori_loop(0, count, look, (jnp.int32(count), jnp.int32(-1)))
    errors[...] = jnp.zeros_like(errors)

    def kern_pair(k):
        pad = jnp.zeros((freq_y, LANES - freq_x), F32)
        return (
            jnp.concatenate([kern_ref[0, k], pad], axis=1),
            jnp.concatenate([kern_ref[1, k], pad], axis=1),
        )

    def work(slot, carry):
        tile = jnp.where(slot == 0, first, last)
        live = jnp.where(slot == 0, first < count, last > first)

        @pl.when(jnp.logical_not(live))
        def _():
            slope_ref[slot] = jnp.zeros(slope_ref.shape[1:], F32)

        @pl.when(live)
        def _():
            one_tile(slot, tile)

        return carry

    def one_tile(slot, tile):
        u = exact(NN, py_ref[...], coeffs_ref[tile])
        u_cos, u_sin = u[:freq_y], u[freq_y:]
        px_cos, px_sin = px_ref[0], px_ref[1]
        spec_re = exact(NT, u_cos, px_cos) - exact(NT, u_sin, px_sin)
        spec_im = -(exact(NT, u_sin, px_cos) + exact(NT, u_cos, px_sin))
        total = jnp.zeros((GRID_X, GRID_Y), F32)
        c_high, c_low = cs_ref[:GRID_X, :], cs_ref[GRID_X:, :]
        for base in range(0, kern, GROUP):
            rows = []
            for k in range(base, base + GROUP):
                h_re, h_im = kern_pair(k)
                f_re = h_re * spec_re - h_im * spec_im
                f_im = h_re * spec_im + h_im * spec_re
                rows.append(jnp.concatenate([f_re, -f_im], axis=1))
                rows.append(jnp.concatenate([f_im, f_re], axis=1))
            f_high, f_low = split(jnp.concatenate(rows, axis=0))
            x_all = nt(f_high, c_high) + (nt(f_high, c_low) + nt(f_low, c_high))
            flipped = [x_all[j * LANES : (j + 1) * LANES].T for j in range(GROUP)]
            x_high, x_low = split(jnp.concatenate(flipped, axis=0))
            amp_all = nn(jnp.concatenate([x_high, x_low, x_high], axis=1), wy_ref[...])
            for j in range(GROUP):
                amp = amp_all[j * GRID_X : (j + 1) * GRID_X]
                amps[base + j] = amp
                re, im = amp[:, :LANES], amp[:, LANES:]
                total = total + weight_ref[base + j] * (re * re + im * im)
        blurred = total
        for _ in range(DIFF_STEPS):
            blurred = diffuse(blurred)
        resist = 1.0 / (1.0 + jnp.exp(-RESIST_SLOPE * (blurred - RESIST_LEVEL)))
        offset = (GRID_X - CORE_X) // 2
        inner = resist[offset : offset + CORE_X]
        target = jnp.concatenate([targets_ref[part, tile] for part in range(PARTS)], axis=0)
        misfit = inner - target.T
        errors[...] += jnp.sum(misfit * misfit, keepdims=True)
        core = (2.0 * RESIST_SLOPE) * misfit * inner * (1.0 - inner)
        edge = jnp.zeros((offset, GRID_Y), F32)
        slope = jnp.concatenate([edge, core, edge], axis=0)
        for _ in range(DIFF_STEPS):
            slope = diffuse(slope)
        slope = 2.0 * slope
        ds_re = jnp.zeros((freq_y, LANES), F32)
        ds_im = jnp.zeros((freq_y, LANES), F32)
        for base in range(0, kern, GROUP):
            grads = []
            for k in range(base, base + GROUP):
                gain = weight_ref[k] * slope
                amp = amps[k]
                grads.append(jnp.concatenate([gain * amp[:, :LANES], gain * amp[:, LANES:]], axis=1))
            d_high, d_low = split(jnp.concatenate(grads, axis=0))
            both = nt(d_high, wy_ref[LANES:])
            dx = both[:, :LANES] + (both[:, LANES:] + nt(d_low, wy_ref[:LANES]))
            flipped = [dx[j * GRID_X : (j + 1) * GRID_X].T for j in range(GROUP)]
            x_high, x_low = split(jnp.concatenate(flipped, axis=0))
            df_all = nn(x_high, c_high) + (nn(x_high, c_low) + nn(x_low, c_high))
            for j in range(GROUP):
                df = df_all[j * LANES : (j + 1) * LANES]
                d_re, d_im = df[:freq_y], df[freq_y:]
                f_re = d_re[:, :LANES] + d_im[:, LANES:]
                f_im = d_im[:, :LANES] - d_re[:, LANES:]
                h_re, h_im = kern_pair(base + j)
                ds_re = ds_re + (h_re * f_re + h_im * f_im)
                ds_im = ds_im + (h_re * f_im - h_im * f_re)
        du_cos = exact(NN, ds_re, px_cos) - exact(NN, ds_im, px_sin)
        du_sin = -(exact(NN, ds_re, px_sin) + exact(NN, ds_im, px_cos))
        slope_ref[slot] = exact(TN, py_ref[...], jnp.concatenate([du_cos, du_sin], axis=0))

    lax.fori_loop(0, MOST, work, 0)
    err_ref[...] = errors[...] * (1.0 / (GRID_Y * CORE_X))


def factors(count):
    pair = 2 if count % 2 == 0 else 1
    rest = count // pair
    inner = max(d for d in range(1, rest + 1) if rest % d == 0 and d * d <= rest)
    return rest // inner, inner, pair


def wrapped(index, size):
    return lax.rem(index + size, size)


class Place:
    def __init__(self, count):
        self.count = count
        self.outer, self.inner, self.pair = factors(count)
        self.me = lax.axis_index("tile")
        self.c = lax.rem(self.me, self.pair)
        self.b = lax.rem(self.me // self.pair, self.inner)
        self.a = self.me // (self.pair * self.inner)

    def at(self, da, db, dc):
        a = wrapped(self.a + da, self.outer)
        b = wrapped(self.b + db, self.inner)
        c = wrapped(self.c + dc, self.pair)
        return (a * self.inner + b) * self.pair + c

    def partners(self):
        return (
            [self.at(d, 0, 0) for d in range(1, self.outer)]
            + [self.at(0, d, 0) for d in range(1, self.inner)]
            + [self.at(0, 0, d) for d in range(1, self.pair)]
        )


def meet(devices):
    barrier = pltpu.get_barrier_semaphore()
    for device in devices:
        pl.semaphore_signal(
            barrier, inc=1, device_id={"tile": device}, device_id_type=pl.DeviceIdType.MESH
        )
    pl.semaphore_wait(barrier, len(devices))


class Gather:
    def __init__(self, place, slots, send, recv):
        self.place, self.slots, self.send, self.recv = place, slots, send, recv
        self.started = []

    def copy(self, slot, device, index):
        return pltpu.make_async_remote_copy(
            src_ref=self.slots.at[slot],
            dst_ref=self.slots.at[slot],
            send_sem=self.send.at[index],
            recv_sem=self.recv.at[slot],
            device_id={"tile": device},
            device_id_type=pl.DeviceIdType.MESH,
        )

    def push(self, slot, device):
        copy = self.copy(slot, device, len(self.started))
        copy.start()
        self.started.append(copy)

    def arrive(self, slot):
        self.copy(slot, self.place.at(1, 0, 0), 0).wait_recv()

    def to_pair(self, slot):
        for d in range(1, self.place.pair):
            self.push(slot, self.place.at(0, 0, d))

    def to_inner(self, slot):
        for d in range(1, self.place.inner):
            self.push(slot, self.place.at(0, d, 0))

    def own(self):
        p = self.place
        for d in range(1, p.outer):
            self.push(p.me, p.at(d, 0, 0))
        self.to_inner(p.me)
        self.to_pair(p.me)

    def outer_arrivals(self):
        for d in range(1, self.place.outer):
            slot = self.place.at(-d, 0, 0)
            self.arrive(slot)
            self.to_inner(slot)
            self.to_pair(slot)

    def inner_arrivals(self):
        for d in range(self.place.outer):
            for e in range(1, self.place.inner):
                slot = self.place.at(-d, -e, 0)
                self.arrive(slot)
                self.to_pair(slot)

    def finish(self):
        p = self.place
        for d in range(p.outer):
            for e in range(p.inner):
                for f in range(1, p.pair):
                    self.arrive(p.at(-d, -e, -f))
        for copy in self.started:
            copy.wait_send()


def spread_kernel(
    count, piece_ref, target_ref, coeff_ref, all_target_ref, near, near_send, near_recv,
    send_c, recv_c, *sems,
):
    place = Place(count)
    me = place.me
    right, left = wrapped(me + 1, count), wrapped(me - 1, count)
    coeff = Gather(place, coeff_ref, send_c, recv_c)
    targets = []
    for part in range(PARTS):
        targets.append(Gather(place, all_target_ref.at[part], sems[2 * part], sems[2 * part + 1]))
        all_target_ref[part, me] = target_ref[part]
    meet([right, left] + place.partners())
    sides = []
    for side, device in ((0, right), (1, left)):
        copy = pltpu.make_async_remote_copy(
            src_ref=piece_ref.at[1 + side],
            dst_ref=near.at[side],
            send_sem=near_send.at[side],
            recv_sem=near_recv.at[side],
            device_id={"tile": device},
            device_id_type=pl.DeviceIdType.MESH,
        )
        copy.start()
        sides.append(copy)
    for target in targets:
        target.own()
    for copy in sides:
        copy.wait()
    own = piece_ref[0]
    own = own + jnp.where(me > 0, near[0], 0.0)
    own = own + jnp.where(me < count - 1, near[1], 0.0)
    coeff_ref[me] = own
    coeff.own()
    forward(targets + [coeff])


def collect_kernel(count, slope_ref, all_ref, *sems):
    place = Place(count)
    gathers = [
        Gather(place, all_ref.at[slot], sems[2 * slot], sems[2 * slot + 1]) for slot in range(MOST)
    ]
    for slot in range(MOST):
        all_ref[slot, place.me] = slope_ref[slot]
    meet(place.partners())
    together(gathers)


def together(gathers):
    for gather in gathers:
        gather.own()
    forward(gathers)


def forward(gathers):
    for gather in gathers:
        gather.outer_arrivals()
    for gather in gathers:
        gather.inner_arrivals()
    for gather in gathers:
        gather.finish()


def tables(tile_px, freq_y, freq_x):
    win = tile_px + 2 * AMBIT
    row = np.zeros((tile_px, ROWS))
    row[:, : freq_y + 1] = real_basis(tile_px, freq_y)
    col = np.zeros((win, LANES))
    col[:, : freq_x + 1] = real_basis(win, freq_x)
    pieces = np.zeros((tile_px, 3 * LANES))
    pieces[:, :LANES] = col[AMBIT : AMBIT + tile_px]
    pieces[tile_px - AMBIT :, LANES : 2 * LANES] = col[:AMBIT]
    pieces[:AMBIT, 2 * LANES :] = col[AMBIT + tile_px :]
    r_high, r_low = halves(row)
    row_fwd = np.concatenate([r_high.T, r_low.T], axis=0)
    row_bwd = np.concatenate([r_high, r_low, r_high], axis=1)
    col_tab = np.stack(halves(pieces))
    py = np.concatenate(pickers(freq_y, freq_y, 72), axis=0)
    px = np.stack(pickers(freq_x, LANES, LANES))
    ax = angle(GRID_X, np.arange(GRID_X), np.arange(freq_x) - freq_x // 2)
    cs = np.zeros((GRID_X, 2 * LANES))
    cs[:, :freq_x] = np.cos(ax)
    cs[:, LANES : LANES + freq_x] = np.sin(ax)
    cs = np.concatenate(halves(cs), axis=0)
    ay = angle(GRID_Y, np.arange(freq_y) - freq_y // 2, np.arange(GRID_Y))
    wy = np.block([[np.cos(ay), np.sin(ay)], [-np.sin(ay), np.cos(ay)]]) / (64.0 * GRID_Y * GRID_X)
    w_high, w_low = halves(wy)
    wy = np.concatenate([w_high, w_high, w_low], axis=0)
    return row_fwd, row_bwd, col_tab, py, px, cs, wy


def whole(shape, memory_space=None):
    return pl.BlockSpec(shape, lambda *_: (0,) * len(shape))


def on_device(mask_tiles, target_grid, kernels, kern_weight, owner_list):
    tile_px = mask_tiles.shape[1]
    kern, freq_y, freq_x = kernels.shape[2:]
    count = lax.axis_size("tile")
    row_fwd, row_bwd, col_tab, py, px, cs, wy = tables(tile_px, freq_y, freq_x)

    chunk = 256
    steps = tile_px // chunk
    pieces = pl.pallas_call(
        coeffs_kernel,
        grid=(steps,),
        in_specs=[
            pl.BlockSpec((1, chunk, tile_px), lambda i: (0, i, 0)),
            pl.BlockSpec((2 * ROWS, chunk), lambda i: (0, i)),
            whole(col_tab.shape),
        ],
        out_specs=whole((3, 72, LANES)),
        out_shape=jax.ShapeDtypeStruct((3, 72, LANES), F32),
        scratch_shapes=[pltpu.VMEM((ROWS, tile_px), F32)],
        compiler_params=pltpu.CompilerParams(vmem_limit_bytes=VMEM_BYTES),
        name="coeffs",
    )(mask_tiles, row_fwd, col_tab)

    vmem = pl.BlockSpec(memory_space=pltpu.VMEM)
    dma = pltpu.SemaphoreType.DMA
    coeffs, targets = pl.pallas_call(
        functools.partial(spread_kernel, count),
        in_specs=[vmem, vmem],
        out_specs=[vmem, vmem],
        out_shape=[
            jax.ShapeDtypeStruct((count, 72, LANES), F32),
            jax.ShapeDtypeStruct((PARTS, count, GRID_Y // PARTS, CORE_X), F32),
        ],
        scratch_shapes=[pltpu.VMEM((2, 72, LANES), F32), dma((2,)), dma((2,))]
        + [dma((count,))] * (2 + 2 * PARTS),
        compiler_params=pltpu.CompilerParams(
            collective_id=0, has_side_effects=True, vmem_limit_bytes=VMEM_BYTES
        ),
        name="spread",
    )(pieces, target_grid.reshape(PARTS, GRID_Y // PARTS, CORE_X))

    smem = pl.BlockSpec(memory_space=pltpu.SMEM)
    owners = owner_list[:, 0]
    slopes, errors = pl.pallas_call(
        owner_kernel,
        in_specs=[smem, smem] + [vmem] * 7,
        out_specs=[vmem, vmem],
        out_shape=[
            jax.ShapeDtypeStruct((MOST, 72, LANES), F32),
            jax.ShapeDtypeStruct((1, 1), F32),
        ],
        scratch_shapes=[
            pltpu.VMEM((kern, GRID_X, 2 * GRID_Y), F32),
            pltpu.VMEM((1, 1), F32),
        ],
        compiler_params=pltpu.CompilerParams(vmem_limit_bytes=VMEM_BYTES),
        name="owner",
    )(owners, kern_weight, coeffs, targets, kernels[0], py, px, cs, wy)

    gathered = pl.pallas_call(
        functools.partial(collect_kernel, count),
        in_specs=[vmem],
        out_specs=vmem,
        out_shape=jax.ShapeDtypeStruct((MOST, count, 72, LANES), F32),
        scratch_shapes=[dma((count,))] * (2 * MOST),
        compiler_params=pltpu.CompilerParams(
            collective_id=1, has_side_effects=True, vmem_limit_bytes=VMEM_BYTES
        ),
        name="collect",
    )(slopes)
    out = pl.pallas_call(
        update_kernel,
        grid=(steps,),
        in_specs=[
            pl.BlockSpec((1, chunk, tile_px), lambda i: (0, i, 0)),
            smem,
            whole((MOST, count, 72, LANES)),
            pl.BlockSpec((chunk, 3 * ROWS), lambda i: (i, 0)),
            whole(col_tab.shape),
        ],
        out_specs=pl.BlockSpec((1, chunk, tile_px), lambda i: (0, i, 0)),
        out_shape=jax.ShapeDtypeStruct(mask_tiles.shape, F32),
        scratch_shapes=[pltpu.VMEM((3 * ROWS, tile_px), BF16)],
        compiler_params=pltpu.CompilerParams(vmem_limit_bytes=VMEM_BYTES),
        name="update",
    )(mask_tiles, owners, gathered, row_bwd, col_tab)
    return out, errors.reshape(1)


def solution(mesh):
    placed = (
        P(("stripe", "tile"), None, None),
        P(("stripe", "tile"), None),
        P("tile", None, None, None, None),
        P(),
        P("stripe", None),
    )
    return jax.shard_map(
        on_device,
        mesh=mesh,
        in_specs=placed,
        out_specs=(P(("stripe", "tile"), None, None), P(("stripe", "tile"))),
        check_vma=False,
    )
```
